32 devices in a mesh: dp: 4 (over z), node: 4 (over x, core), local: 2 (over y).
Axes of the slice: x: 2, y: 2, z: 4, core: 2. Of those that a mesh axis runs over, the one named last changes fastest.
Arguments:
- d_out: bfloat16 [2048, 7168], P(('dp', 'node'), 'local'), may hold values from -6 to 6
- logits: float32 [2048, 4], P(('dp', 'node')), may hold values from -6 to 6
- groups: int32 [2048, 2], P(('dp', 'node')), may hold values from 0 to 3, as said below
- slots: int32 [2048, 2], P(('dp', 'node')), may hold values from -1 to 71, as said below
- hidden_act: bfloat16 [4, 4, 4, 72, 1024], P('dp', 'node'), may hold values from -6 to 6
- w_down: bfloat16 [4, 1024, 7168], P('node', None, 'local'), may hold values from -0.1875 to 0.1875
Outputs:
- d_logits: float32 [2048, 4], P(('dp', 'node'))
- d_hidden: bfloat16 [4, 4, 4, 72, 1024], P('dp', 'node', None, None, 'local')
- d_wdown: bfloat16 [4, 1024, 7168], P('node', 'dp', 'local')
The draws below stay inside these ranges and needn't reach their ends.
Inputs may be any that keep to these rules, and one draw needn't show every extreme that they name: `groups`: each row names 2 different experts. `slots`: a live route's slot is its rank among the routes to that expert of the 128 rows of its source device, counted in order of token and then of position in the row; routes whose rank reaches 72 are dropped and hold -1.
All inputs are finite; a program needn't handle non-finite values.
Results may differ from the reference program's by a relative error of at most 0.009.
Values may be sent and summed in bfloat16 or wider, within the bound.
A program may use at most 64 MiB of HBM per device.

```python
import jax
import jax.numpy as jnp
from jax import lax

D = 7168
HID = 1024
TOK_DEV = 128
TOPG = 2
EXPERTS = 4
CAP = 72
TOKENS = 2048
N_DP = 4
N_NODE = 4


def routing(key):
    blocks = TOKENS // TOK_DEV
    key_noise, key_bias, key_heavy = jax.random.split(key, 3)
    noise = jax.random.randint(key_noise, (blocks, TOK_DEV, EXPERTS), 0, 1000)
    bias = jax.random.randint(key_bias, (blocks, 1, EXPERTS), 0, 700)
    heavy = jax.random.randint(key_heavy, (blocks, 1, 1), 0, EXPERTS)
    columns = jnp.arange(EXPERTS, dtype=jnp.int32)[None, None, :]
    score = noise + bias + jnp.where(columns == heavy, 100000, 0)
    score = score * EXPERTS + columns
    _, chosen = lax.top_k(score, TOPG)
    chosen = chosen.astype(jnp.int32)
    flat = chosen.reshape(blocks, TOK_DEV * TOPG)
    onehot = (flat[..., None] == jnp.arange(EXPERTS, dtype=jnp.int32)).astype(jnp.int32)
    ranks = jnp.cumsum(onehot, axis=1) - 1
    rank = jnp.sum(ranks * onehot, axis=-1)
    placed = jnp.where(rank < CAP, rank, -1).astype(jnp.int32)
    return (chosen.reshape(TOKENS, TOPG), placed.reshape(TOKENS, TOPG))


def draw_groups(key, part):
    chosen, placed = routing(key)
    return chosen


def draw_slots(key, part):
    chosen, placed = routing(key)
    return placed


def block_levels(stream_key, extent, cuts, smallest, largest):
    loudness, own = 1.0, jax.random.fold_in(stream_key, 6)
    for dim, blocks in cuts:
        heights = jnp.exp(jax.random.uniform(jax.random.fold_in(own, dim), (blocks,), jnp.float32, smallest / len(cuts), largest / len(cuts)))
        loudness = loudness * jnp.repeat(heights, extent[dim] // blocks).reshape([-1 if axis == dim else 1 for axis in range(len(extent))])
    return loudness


def normal_values(rng, dims, deviation, reach, cuts=(), kind=jnp.bfloat16):
    gain = block_levels(rng, dims, cuts, -0.22, 0.18) if cuts else 1.0
    drawn = jax.random.normal(rng, dims, jnp.float32) * deviation * gain
    return jnp.minimum(jnp.maximum(drawn, -reach), reach).astype(kind)


def setup_inputs(seed: int = 0) -> dict:
    arg_keys = jax.random.split(jax.random.key(seed), 7)
    d_out = normal_values(arg_keys[0], (TOKENS, D), 1.0, 6.0, ((0, 16), (1, 2)))
    logits = normal_values(arg_keys[1], (TOKENS, EXPERTS), 1.5, 6.0, ((0, 16),), jnp.float32)
    groups = draw_groups(jax.random.fold_in(arg_keys[6], 71), 0)
    slots = draw_slots(jax.random.fold_in(arg_keys[6], 71), 0)
    hidden_act = normal_values(arg_keys[4], (N_DP, EXPERTS, N_NODE, CAP, HID), 1.0, 6.0, ((0, 4), (1, 4)))
    w_down = normal_values(arg_keys[5], (EXPERTS, HID, D), HID ** -0.5, 0.1875, ((0, 4), (2, 2)))
    return {"d_out": d_out, "logits": logits, "groups": groups, "slots": slots, "hidden_act": hidden_act, "w_down": w_down}


route_scale = 2.5

def route_tables(logits, groups, slots, cap_rows):
    expert_count = logits.shape[1]
    scores = jax.nn.sigmoid(logits)
    picked = (groups[..., None] == jnp.arange(expert_count, dtype=jnp.int32)).astype(jnp.float32)
    chosen = lax.optimization_barrier(jnp.sum(picked * scores[:, None, :], axis=-1))
    totals = lax.optimization_barrier(jnp.sum(chosen, axis=-1, keepdims=True))
    gates = (route_scale * chosen / totals).astype(jnp.bfloat16)
    target = jnp.where(slots >= 0, groups * cap_rows + slots, -1).astype(jnp.int32)
    placed = (target[..., None] == jnp.arange(expert_count * cap_rows, dtype=jnp.int32)).astype(jnp.float32)
    return (picked, chosen, totals, gates, placed)

def logit_grad(picked, chosen, totals, route_dot):
    shares = chosen / totals
    mean_dot = lax.optimization_barrier(jnp.sum(shares * route_dot, axis=-1, keepdims=True))
    d_chosen = route_scale * (route_dot - mean_dot) / totals
    return jnp.einsum('tke,tk->te', picked, d_chosen * chosen * (1.0 - chosen))

def reference(d_out, logits, groups, slots, hidden_act, w_down):
    picked, chosen, totals, gates, placed = route_tables(logits, groups, slots, CAP)
    group_rows = N_NODE * TOK_DEV
    width = d_out.shape[1]
    placed_blocks = placed.reshape(N_DP, N_NODE, TOK_DEV, TOPG, EXPERTS * CAP)
    gate_blocks = gates.astype(jnp.float32).reshape(N_DP, N_NODE, TOK_DEV, TOPG)
    out_blocks = d_out.reshape(N_DP, N_NODE, TOK_DEV, width)

    def one_group(carry, index):
        placed_here = lax.dynamic_index_in_dim(placed_blocks, index, 0, False)
        gate_here = lax.dynamic_index_in_dim(gate_blocks, index, 0, False)
        out_here = lax.dynamic_index_in_dim(out_blocks, index, 0, False).astype(jnp.float32)
        acts = lax.dynamic_index_in_dim(hidden_act, index, 0, False)
        sent = jnp.einsum('stkc,std->scd', placed_here, out_here, precision=lax.Precision.HIGHEST).astype(jnp.bfloat16)
        sent_gate = jnp.einsum('stkc,stk->sc', placed_here, gate_here, precision=lax.Precision.HIGHEST)
        sent = sent.reshape(N_NODE, EXPERTS, CAP, width).transpose(1, 0, 2, 3).reshape(EXPERTS, N_NODE * CAP, width)
        sent_gate = sent_gate.reshape(N_NODE, EXPERTS, CAP).transpose(1, 0, 2).reshape(EXPERTS, N_NODE * CAP)

        def one_expert(items):
            rows, row_gate, act_rows, weight = items
            act_rows = act_rows.reshape(N_NODE * CAP, HID)
            expert_out = jnp.dot(act_rows, weight, preferred_element_type=jnp.float32)
            dots = lax.optimization_barrier(jnp.sum(rows.astype(jnp.float32) * expert_out, axis=-1))
            back = jnp.dot(rows, weight.T, preferred_element_type=jnp.float32)
            grad_hidden = (row_gate[:, None] * back).astype(jnp.bfloat16)
            scaled = (row_gate[:, None] * rows.astype(jnp.float32)).astype(jnp.bfloat16)
            part = jnp.dot(act_rows.T, scaled, preferred_element_type=jnp.float32).astype(jnp.bfloat16)
            return (dots, grad_hidden, part)
        dots, grad_hidden, parts = lax.map(one_expert, (sent, sent_gate, acts, w_down))
        return (carry + parts.astype(jnp.float32), (dots, grad_hidden))
    start = jnp.zeros((EXPERTS, HID, width), jnp.float32)
    summed, (dots, grad_hidden) = lax.scan(one_group, start, jnp.arange(N_DP, dtype=jnp.int32))
    d_hidden = grad_hidden.reshape(N_DP, EXPERTS, N_NODE, CAP, HID)
    dots = dots.reshape(N_DP, EXPERTS, N_NODE, CAP).transpose(0, 2, 1, 3).reshape(N_DP * N_NODE, EXPERTS * CAP)
    route_dot = jnp.einsum('btkc,bc->btk', placed.reshape(N_DP * N_NODE, TOK_DEV, TOPG, EXPERTS * CAP), dots, precision=lax.Precision.HIGHEST)
    route_dot = route_dot.reshape(group_rows * N_DP, TOPG)
    d_logits = logit_grad(picked, chosen, totals, route_dot)
    return (d_logits, d_hidden, summed.astype(jnp.bfloat16))
```

```python
import functools

import jax
import jax.numpy as jnp
from jax import lax
from jax.experimental import pallas as pl
from jax.experimental.pallas import tpu as pltpu
from jax.sharding import PartitionSpec as P

route_scale = 2.5
gather_limit = 20 * 1024 * 1024
chunk_rows = 32


def peer(**where):
    return dict(device_id=where, device_id_type=pl.DeviceIdType.MESH)


def greet(peers):
    barrier = pltpu.get_barrier_semaphore()
    for where in peers:
        pl.semaphore_signal(barrier, inc=1, **where)
    pl.semaphore_wait(barrier, len(peers))


def node_kernel(nodes, own_ref, out_ref, local_sem, x_send, x_recv, c_send, c_recv):
    node = lax.axis_index("node")
    chips = nodes // 2
    chip, core = node // 2, node % 2
    sibling = chip * 2 + 1 - core
    others = [lax.rem(chip + step, chips) * 2 + core for step in range(1, chips)]
    greet([peer(node=other) for other in others] + [peer(node=sibling)])
    chunks = own_ref.shape[0] // chunk_rows

    keep = pltpu.make_async_copy(own_ref, out_ref.at[node], local_sem)
    keep.start()

    def to_chip(step, k):
        rows = pl.ds(k * chunk_rows, chunk_rows)
        return pltpu.make_async_remote_copy(
            own_ref.at[rows], out_ref.at[node, rows], x_send.at[step - 1, k], x_recv.at[step - 1, k],
            **peer(node=lax.rem(chip + step, chips) * 2 + core))

    def to_core(step, k):
        rows = pl.ds(k * chunk_rows, chunk_rows)
        origin = lax.rem(chip - step + chips, chips) * 2 + core
        source = own_ref.at[rows] if step == 0 else out_ref.at[origin, rows]
        return pltpu.make_async_remote_copy(
            source, out_ref.at[origin, rows], c_send.at[step, k], c_recv.at[step, k], **peer(node=sibling))

    for k in range(chunks):
        for step in range(1, chips):
            to_chip(step, k).start()
    for k in range(chunks):
        to_core(0, k).start()
    for k in range(chunks):
        for step in range(1, chips):
            to_chip(step, k).wait_recv()
            to_core(step, k).start()
    for k in range(chunks):
        for step in range(1, chips):
            to_chip(step, k).wait_send()
        for step in range(chips):
            to_core(step, k).wait()
    keep.wait()


def world_kernel(groups, nodes, own_ref, near_ref, act_ref, out_ref, act_out, local_sems,
                 z_recv, right_send, left_send, x_send, x_recv, c_send, c_recv, a_send, a_recv):
    mine, node = lax.axis_index("dp"), lax.axis_index("node")
    chips = nodes // 2
    chip, core = node // 2, node % 2
    sibling = chip * 2 + 1 - core
    greet([peer(dp=lax.rem(mine + step, groups)) for step in range(1, groups)]
          + [peer(node=lax.rem(chip + step, chips) * 2 + core) for step in range(1, chips)]
          + [peer(node=sibling)])
    chunks = own_ref.shape[0] // chunk_rows
    part = act_out.shape[2]

    def hop(side, source, k, first):
        rows = pl.ds(k * chunk_rows, chunk_rows)
        sems = right_send if side > 0 else left_send
        block = own_ref.at[rows] if first else out_ref.at[source, node, rows]
        return pltpu.make_async_remote_copy(
            block, out_ref.at[source, node, rows], sems.at[source, k], z_recv.at[source, k],
            **peer(dp=mine + side))

    def to_chip(source, step, k):
        rows = pl.ds(k * chunk_rows, chunk_rows)
        return pltpu.make_async_remote_copy(
            out_ref.at[source, node, rows], out_ref.at[source, node, rows],
            x_send.at[source, step - 1, k], x_recv.at[source, step - 1, k],
            **peer(node=lax.rem(chip + step, chips) * 2 + core))

    def to_core(source, step, k):
        rows = pl.ds(k * chunk_rows, chunk_rows)
        origin = lax.rem(chip - step + chips, chips) * 2 + core
        return pltpu.make_async_remote_copy(
            out_ref.at[source, origin, rows], out_ref.at[source, origin, rows],
            c_send.at[source, step, k], c_recv.at[source, step, k], **peer(node=sibling))

    def act_copy(step):
        target = lax.rem(mine + step, groups)
        columns = pl.ds(pl.multiple_of(target * part, part), part)
        return pltpu.make_async_remote_copy(
            act_ref.at[:, columns], act_out.at[mine], a_send.at[step - 1], a_recv.at[step - 1],
            **peer(dp=target))

    for k in range(chunks):
        @pl.when(mine + 1 < groups)
        def _():
            hop(1, mine, k, True).start()

        @pl.when(mine > 0)
        def _():
            hop(-1, mine, k, True).start()

    keep_near = pltpu.make_async_copy(near_ref, out_ref.at[mine], local_sems.at[0])
    keep_near.start()
    own_columns = pl.ds(pl.multiple_of(mine * part, part), part)
    keep_act = pltpu.make_async_copy(act_ref.at[:, own_columns], act_out.at[mine], local_sems.at[1])
    keep_act.start()
    for step in range(1, groups):
        act_copy(step).start()

    def sides(distance):
        return (
            (1, mine - distance, mine - distance >= 0, jnp.logical_and(mine - distance >= 0, mine + 1 < groups)),
            (-1, mine + distance, mine + distance < groups, jnp.logical_and(mine + distance < groups, mine > 0)),
        )

    def spread(distance, k):
        for side, source, here, further in sides(distance):
            @pl.when(here)
            def _():
                hop(side, source, k, False).wait_recv()

            @pl.when(further)
            def _():
                hop(side, source, k, False).start()

            @pl.when(here)
            def _():
                for step in range(1, chips):
                    to_chip(source, step, k).start()
                to_core(source, 0, k).start()

    def pass_on(distance, k):
        for side, source, here, further in sides(distance):
            @pl.when(here)
            def _():
                for step in range(1, chips):
                    to_chip(source, step, k).wait_recv()
                    to_core(source, step, k).start()

    order = [(distance, k) for distance in range(1, groups) for k in range(chunks)]
    for at, item in enumerate(order):
        spread(*item)
        if at >= 2:
            pass_on(*order[at - 2])
    for item in order[-2:]:
        pass_on(*item)

    for distance, k in order:
        for side, source, here, further in sides(distance):
            @pl.when(further)
            def _():
                hop(side, source, k, False).wait_send()

            @pl.when(here)
            def _():
                for step in range(1, chips):
                    to_chip(source, step, k).wait_send()
                for step in range(chips):
                    to_core(source, step, k).wait()
    for k in range(chunks):
        @pl.when(mine + 1 < groups)
        def _():
            hop(1, mine, k, True).wait_send()

        @pl.when(mine > 0)
        def _():
            hop(-1, mine, k, True).wait_send()
    for step in range(1, groups):
        act_copy(step).wait()
    keep_near.wait()
    keep_act.wait()


def anywhere(count):
    return [pl.BlockSpec(memory_space=pl.ANY)] * count


def gather_node(d_out, nodes):
    chunks, chips = d_out.shape[0] // chunk_rows, nodes // 2
    dma = pltpu.SemaphoreType.DMA
    return pl.pallas_call(
        functools.partial(node_kernel, nodes),
        out_shape=jax.ShapeDtypeStruct((nodes,) + d_out.shape, d_out.dtype),
        in_specs=anywhere(1),
        out_specs=pl.BlockSpec(memory_space=pl.ANY),
        scratch_shapes=[dma, dma((chips - 1, chunks)), dma((chips - 1, chunks)), dma((chips, chunks)), dma((chips, chunks))],
        cost_estimate=pl.CostEstimate(flops=0, bytes_accessed=40 << 20, transcendentals=0),
        compiler_params=pltpu.CompilerParams(collective_id=0, has_side_effects=True),
    )(d_out)


def gather_world(d_out, near, act, groups, nodes):
    chunks, chips = d_out.shape[0] // chunk_rows, nodes // 2
    dma = pltpu.SemaphoreType.DMA
    return pl.pallas_call(
        functools.partial(world_kernel, groups, nodes),
        out_shape=(
            jax.ShapeDtypeStruct((groups, nodes) + d_out.shape, d_out.dtype),
            jax.ShapeDtypeStruct((groups, act.shape[0], act.shape[1] // groups), act.dtype),
        ),
        in_specs=anywhere(3),
        out_specs=tuple(anywhere(2)),
        scratch_shapes=[
            dma((2,)), dma((groups, chunks)), dma((groups, chunks)), dma((groups, chunks)),
            dma((groups, chips - 1, chunks)), dma((groups, chips - 1, chunks)),
            dma((groups, chips, chunks)), dma((groups, chips, chunks)),
            dma((groups - 1,)), dma((groups - 1,)),
        ],
        cost_estimate=pl.CostEstimate(flops=0, bytes_accessed=200 << 20, transcendentals=0),
        compiler_params=pltpu.CompilerParams(collective_id=1, has_side_effects=True),
    )(d_out, near, act)


def routing(logits, groups):
    scores = jax.nn.sigmoid(logits)
    picked = (groups[..., None] == jnp.arange(logits.shape[1], dtype=jnp.int32)).astype(jnp.float32)
    chosen = jnp.sum(picked * scores[:, None, :], axis=-1)
    totals = jnp.sum(chosen, axis=-1, keepdims=True)
    return picked, chosen, totals


def gather_shards(d_out, logits, groups, slots, hidden_act, w_down):
    dp_count, node_count = lax.axis_size("dp"), lax.axis_size("node")
    me_dp, me_node, me_local = lax.axis_index("dp"), lax.axis_index("node"), lax.axis_index("local")
    tokens, feat_local = d_out.shape
    cap_rows, hid_units = hidden_act.shape[3], hidden_act.shape[4]
    slot_count = node_count * cap_rows
    group_tokens = node_count * tokens
    act_rows = hidden_act.reshape(slot_count, hid_units)
    weight = w_down.reshape(hid_units, feat_local)

    picked, chosen, totals = routing(logits, groups)
    gates = (route_scale * chosen / totals).astype(jnp.bfloat16).astype(jnp.float32)
    pairs = jnp.concatenate([groups.astype(jnp.float32), slots.astype(jnp.float32), gates], axis=1).T
    pairs = jnp.concatenate([pairs, jnp.zeros((2, tokens), jnp.float32)], axis=0)
    near = gather_node(d_out, node_count)
    facts = lax.all_gather(pairs, ("dp", "node"), axis=0, tiled=False)
    facts = facts.reshape(dp_count, node_count, 8, tokens)
    expert = me_node.astype(jnp.float32)
    live = (facts[:, :, 0:2] == expert) & (facts[:, :, 2:4] >= 0)
    source = jnp.arange(node_count, dtype=jnp.float32)[None, :, None, None] * cap_rows
    where = jnp.sum(jnp.where(live, facts[:, :, 2:4] + source + 1.0, 0.0), axis=2) - 1.0
    where = where.reshape(dp_count, group_tokens).astype(jnp.int32)
    gate = jnp.sum(jnp.where(live, facts[:, :, 4:6], 0.0), axis=2).reshape(dp_count, group_tokens)

    own_where = lax.dynamic_index_in_dim(where, me_dp, 0, keepdims=False)
    own_gate = lax.dynamic_index_in_dim(gate, me_dp, 0, keepdims=False)
    fills = jnp.arange(slot_count, dtype=jnp.int32)[:, None] == own_where[None, :]
    rows = jnp.dot(
        fills.astype(jnp.bfloat16), near.reshape(group_tokens, feat_local), preferred_element_type=jnp.float32
    ).astype(jnp.bfloat16)
    row_gate = jnp.sum(jnp.where(fills, own_gate[None, :], 0.0), axis=1)
    term = lax.dot_general(rows, weight, (((1,), (1,)), ((), ())), preferred_element_type=jnp.float32)
    dot_part = jnp.sum(act_rows.astype(jnp.float32) * term, axis=1)
    half = hid_units // 2
    gated = row_gate[:, None] * term
    away = lax.dynamic_slice_in_dim(gated, (1 - me_local) * half, half, axis=1).astype(jnp.bfloat16)
    home = lax.dynamic_slice_in_dim(gated, me_local * half, half, axis=1)
    come = lax.ppermute(away, "local", [(0, 1), (1, 0)])
    d_hidden = (home + come.astype(jnp.float32)).astype(jnp.bfloat16)
    d_hidden = d_hidden.reshape(1, 1, node_count, cap_rows, half)

    token_dot = jnp.sum(jnp.where(fills, dot_part[:, None], 0.0), axis=0)
    is_mine = (jnp.arange(node_count) == me_node)[:, None]
    all_dots = lax.psum(jnp.where(is_mine, token_dot[None, :], 0.0), ("node", "local"))

    world, acts = gather_world(d_out, near, act_rows, dp_count, node_count)
    spots = (where[:, :, None] == jnp.arange(slot_count, dtype=jnp.int32)).astype(jnp.bfloat16)
    spots = spots * gate.astype(jnp.bfloat16)[:, :, None]
    left = jnp.einsum("dtc,dch->dth", spots, acts, preferred_element_type=jnp.float32).astype(jnp.bfloat16)
    d_wdown = lax.dot_general(
        left.reshape(dp_count * group_tokens, -1), world.reshape(dp_count * group_tokens, feat_local),
        (((0,), (0,)), ((), ())), preferred_element_type=jnp.float32,
    ).astype(jnp.bfloat16)
    d_wdown = d_wdown.reshape((1,) + d_wdown.shape)

    my_dots = lax.dynamic_slice_in_dim(all_dots, me_node * tokens, tokens, axis=1).T
    route_dot = jnp.sum(picked * my_dots[:, None, :], axis=-1)
    return (logit_grads(picked, chosen, totals, route_dot), d_hidden, d_wdown)


def logit_grads(picked, chosen, totals, route_dot):
    mean_dot = jnp.sum(chosen / totals * route_dot, axis=-1, keepdims=True)
    d_chosen = route_scale * (route_dot - mean_dot) / totals
    return jnp.sum(picked * (d_chosen * chosen * (1.0 - chosen))[..., None], axis=1)


def shards(d_out, logits, groups, slots, hidden_act, w_down):
    node_count = lax.axis_size("node")
    expert_count = logits.shape[1]
    cap_rows = hidden_act.shape[3]
    hid_units = hidden_act.shape[4]
    feat_local = d_out.shape[1]
    scores = jax.nn.sigmoid(logits)
    picked = (groups[..., None] == jnp.arange(expert_count, dtype=jnp.int32)).astype(jnp.float32)
    chosen = jnp.sum(picked * scores[:, None, :], axis=-1)
    totals = jnp.sum(chosen, axis=-1, keepdims=True)
    gates = (route_scale * chosen / totals).astype(jnp.bfloat16)
    target = jnp.where(slots >= 0, groups * cap_rows + slots, -1)
    placed = (target[..., None] == jnp.arange(expert_count * cap_rows, dtype=jnp.int32)).astype(
        jnp.float32
    )
    send_rows = jnp.einsum(
        "tkc,td->cd", placed.astype(jnp.bfloat16), d_out, preferred_element_type=jnp.float32
    )
    send_rows = send_rows.astype(jnp.bfloat16).reshape(expert_count, cap_rows, feat_local)
    send_gates = jnp.einsum(
        "tkc,tk->c", placed, gates.astype(jnp.float32), precision=lax.Precision.HIGHEST
    )
    send_gates = send_gates.astype(jnp.bfloat16).reshape(expert_count, cap_rows)
    recv_rows, recv_gates = (
        lax.all_to_all(send_rows, "node", split_axis=0, concat_axis=0, tiled=True),
        lax.all_to_all(send_gates, "node", split_axis=0, concat_axis=0, tiled=True),
    )
    rows = recv_rows.reshape(node_count * cap_rows, feat_local)
    row_gate = recv_gates.reshape(node_count * cap_rows).astype(jnp.float32)
    act_rows = hidden_act.reshape(node_count * cap_rows, hid_units)
    weight = w_down.reshape(hid_units, feat_local)
    expert_out = jnp.dot(act_rows, weight, preferred_element_type=jnp.float32)
    dot_part = jnp.sum(rows.astype(jnp.float32) * expert_out, axis=-1)
    term = lax.dot_general(
        weight, rows, (((1,), (1,)), ((), ())), preferred_element_type=jnp.float32
    )
    summed = lax.psum_scatter(
        (term * row_gate[None, :]).astype(jnp.bfloat16), "local", scatter_dimension=0, tiled=True
    ).astype(jnp.float32)
    d_hidden = summed.T.astype(jnp.bfloat16).reshape(1, 1, node_count, cap_rows, summed.shape[0])
    scaled = (row_gate[:, None] * rows.astype(jnp.float32)).astype(jnp.bfloat16)
    weight_term = lax.dot_general(
        act_rows, scaled, (((0,), (0,)), ((), ())), preferred_element_type=jnp.float32
    )
    weight_sum = lax.psum_scatter(
        weight_term.astype(jnp.bfloat16), "dp", scatter_dimension=0, tiled=True
    ).astype(jnp.float32)
    d_wdown = weight_sum.astype(jnp.bfloat16).reshape(1, weight_sum.shape[0], feat_local)
    outgoing = lax.psum(dot_part, "local")
    returned = lax.all_to_all(
        outgoing.reshape(node_count, cap_rows), "node", split_axis=0, concat_axis=0, tiled=True
    ).reshape(node_count * cap_rows)
    route_dot = jnp.einsum("tkc,c->tk", placed, returned, precision=lax.Precision.HIGHEST)
    shares = chosen / totals
    mean_dot = jnp.sum(shares * route_dot, axis=-1, keepdims=True)
    d_chosen = route_scale * (route_dot - mean_dot) / totals
    d_logits = jnp.einsum("tke,tk->te", picked, d_chosen * chosen * (1.0 - chosen))
    return (d_logits, d_hidden, d_wdown)


def solution(mesh):
    in_specs = (
        P(("dp", "node"), "local"),
        P(("dp", "node"), None),
        P(("dp", "node"), None),
        P(("dp", "node"), None),
        P("dp", "node", None, None, None),
        P("node", None, "local"),
    )
    out_specs = (
        P(("dp", "node"), None),
        P("dp", "node", None, None, "local"),
        P("node", "dp", "local"),
    )

    def run(d_out, *rest):
        gathered = d_out.shape[0] * d_out.shape[1] // mesh.shape["local"] * d_out.dtype.itemsize
        fits = gathered <= gather_limit and mesh.shape["local"] == 2 and rest[0].shape[1] == mesh.shape["node"]
        body = gather_shards if fits else shards
        return jax.shard_map(body, mesh=mesh, in_specs=in_specs, out_specs=out_specs, check_vma=False)(d_out, *rest)

    return run
```

```python
import functools

import jax
import jax.numpy as jnp
from jax import lax
from jax.experimental import pallas as pl
from jax.experimental.pallas import tpu as pltpu
from jax.sharding import PartitionSpec as P

route_scale = 2.5
gather_limit = 20 * 1024 * 1024
chunk_rows = 32
pass_lag = 3


def peer(**where):
    return dict(device_id=where, device_id_type=pl.DeviceIdType.MESH)


def greet(peers):
    barrier = pltpu.get_barrier_semaphore()
    for where in peers:
        pl.semaphore_signal(barrier, inc=1, **where)
    pl.semaphore_wait(barrier, len(peers))


def world_kernel(groups, nodes, own_ref, act_ref, facts_ref, out_ref, act_out, facts_out, stage, local_sems,
                 z_recv, right_send, left_send, x_send, x_recv, c_send, c_recv, a_send, a_recv, f_send, f_recv):
    mine, node = lax.axis_index("dp"), lax.axis_index("node")
    chips = nodes // 2
    chip, core = node // 2, node % 2
    sibling = chip * 2 + 1 - core
    world = groups * nodes
    everyone = []
    for step in range(1, world):
        other = lax.rem(mine * nodes + node + step, world)
        everyone.append(peer(dp=other // nodes, node=other % nodes))
    greet(everyone)
    chunks = own_ref.shape[0] // chunk_rows
    part = act_out.shape[2]

    def block(source, origin, k):
        return out_ref.at[source, origin, pl.ds(k * chunk_rows, chunk_rows)]

    def own(k):
        return own_ref.at[pl.ds(k * chunk_rows, chunk_rows)]

    def hop(side, source, k, first):
        sems = right_send if side > 0 else left_send
        return pltpu.make_async_remote_copy(
            own(k) if first else block(source, node, k), block(source, node, k),
            sems.at[source, k], z_recv.at[source, k], **peer(dp=mine + side))

    def to_chip(source, step, k, first):
        return pltpu.make_async_remote_copy(
            own(k) if first else block(source, node, k), block(source, node, k),
            x_send.at[source, step - 1, k], x_recv.at[source, step - 1, k],
            **peer(node=lax.rem(chip + step, chips) * 2 + core))

    def to_core(source, step, k, first):
        origin = lax.rem(chip - step + chips, chips) * 2 + core
        return pltpu.make_async_remote_copy(
            own(k) if first and step == 0 else block(source, origin, k), block(source, origin, k),
            c_send.at[source, step, k], c_recv.at[source, step, k], **peer(node=sibling))

    def act_copy(step):
        target = lax.rem(mine + step, groups)
        columns = pl.ds(pl.multiple_of(target * part, part), part)
        return pltpu.make_async_remote_copy(
            act_ref.at[:, columns], act_out.at[mine], a_send.at[step - 1], a_recv.at[step - 1],
            **peer(dp=target))

    def fact_copy(step):
        return pltpu.make_async_remote_copy(
            facts_ref, facts_out.at[mine, node], f_send.at[step - 1], f_recv.at[step - 1], **everyone[step - 1])

    def sides(distance):
        return (
            (1, mine - distance, mine - distance >= 0, jnp.logical_and(mine - distance >= 0, mine + 1 < groups)),
            (-1, mine + distance, mine + distance < groups, jnp.logical_and(mine + distance < groups, mine > 0)),
        )

    def spread(distance, k):
        if distance == 0:
            for side, source, here, further in sides(0):
                @pl.when(further)
                def _():
                    hop(side, source, k, True).start()
            for step in range(1, chips):
                to_chip(mine, step, k, True).start()
            to_core(mine, 0, k, True).start()
            return
        for side, source, here, further in sides(distance):
            @pl.when(here)
            def _():
                hop(side, source, k, False).wait_recv()

            @pl.when(further)
            def _():
                hop(side, source, k, False).start()

            @pl.when(here)
            def _():
                for step in range(1, chips):
                    to_chip(source, step, k, False).start()
                to_core(source, 0, k, False).start()

    def pass_on(distance, k):
        for side, source, here, further in sides(distance)[:1 if distance == 0 else 2]:
            @pl.when(here)
            def _():
                for step in range(1, chips):
                    to_chip(source, step, k, distance == 0).wait_recv()
                    to_core(source, step, k, distance == 0).start()

    fetch = pltpu.make_async_copy(own_ref, stage, local_sems.at[0])
    fetch.start()
    own_columns = pl.ds(pl.multiple_of(mine * part, part), part)
    keep_act = pltpu.make_async_copy(act_ref.at[:, own_columns], act_out.at[mine], local_sems.at[1])
    keep_act.start()
    keep_facts = pltpu.make_async_copy(facts_ref, facts_out.at[mine, node], local_sems.at[2])
    keep_facts.start()
    for k in range(chunks):
        spread(0, k)
    for step in range(1, groups):
        act_copy(step).start()
    for step in range(1, world):
        fact_copy(step).start()
    fetch.wait()
    keep = pltpu.make_async_copy(stage, out_ref.at[mine, node], local_sems.at[0])
    keep.start()

    order = [(distance, k) for distance in range(groups) for k in range(chunks)]
    for at in range(chunks, len(order) + pass_lag):
        if at < len(order):
            spread(*order[at])
        if at == chunks:
            for item in order[:chunks - pass_lag]:
                pass_on(*item)
        pass_on(*order[at - pass_lag])

    for distance, k in order:
        for side, source, here, further in sides(distance):
            @pl.when(further)
            def _():
                hop(side, source, k, distance == 0).wait_send()

        for side, source, here, further in sides(distance)[:1 if distance == 0 else 2]:
            @pl.when(here)
            def _():
                for step in range(1, chips):
                    to_chip(source, step, k, distance == 0).wait_send()
                for step in range(chips):
                    to_core(source, step, k, distance == 0).wait()
    for step in range(1, groups):
        act_copy(step).wait()
    for step in range(1, world):
        fact_copy(step).wait()
    keep.wait()
    keep_act.wait()
    keep_facts.wait()


def anywhere(count):
    return [pl.BlockSpec(memory_space=pl.ANY)] * count


def gather_world(d_out, act, facts, groups, nodes):
    chunks, chips = d_out.shape[0] // chunk_rows, nodes // 2
    dma = pltpu.SemaphoreType.DMA
    return pl.pallas_call(
        functools.partial(world_kernel, groups, nodes),
        out_shape=(
            jax.ShapeDtypeStruct((groups, nodes) + d_out.shape, d_out.dtype),
            jax.ShapeDtypeStruct((groups, act.shape[0], act.shape[1] // groups), act.dtype),
            jax.ShapeDtypeStruct((groups, nodes) + facts.shape, facts.dtype),
        ),
        in_specs=anywhere(3),
        out_specs=tuple(anywhere(3)),
        scratch_shapes=[
            pltpu.VMEM(d_out.shape, d_out.dtype),
            dma((3,)), dma((groups, chunks)), dma((groups, chunks)), dma((groups, chunks)),
            dma((groups, chips - 1, chunks)), dma((groups, chips - 1, chunks)),
            dma((groups, chips, chunks)), dma((groups, chips, chunks)),
            dma((groups - 1,)), dma((groups - 1,)),
            dma((groups * nodes - 1,)), dma((groups * nodes - 1,)),
        ],
        cost_estimate=pl.CostEstimate(flops=0, bytes_accessed=200 << 20, transcendentals=0),
        compiler_params=pltpu.CompilerParams(collective_id=0, has_side_effects=True),
    )(d_out, act, facts)


def routing(logits, groups):
    scores = jax.nn.sigmoid(logits)
    picked = (groups[..., None] == jnp.arange(logits.shape[1], dtype=jnp.int32)).astype(jnp.float32)
    chosen = jnp.sum(picked * scores[:, None, :], axis=-1)
    totals = jnp.sum(chosen, axis=-1, keepdims=True)
    return picked, chosen, totals


def gather_shards(d_out, logits, groups, slots, hidden_act, w_down):
    dp_count, node_count = lax.axis_size("dp"), lax.axis_size("node")
    me_dp, me_node, me_local = lax.axis_index("dp"), lax.axis_index("node"), lax.axis_index("local")
    tokens, feat_local = d_out.shape
    cap_rows, hid_units = hidden_act.shape[3], hidden_act.shape[4]
    slot_count = node_count * cap_rows
    group_tokens = node_count * tokens
    act_rows = hidden_act.reshape(slot_count, hid_units)
    weight = w_down.reshape(hid_units, feat_local)

    picked, chosen, totals = routing(logits, groups)
    gates = (route_scale * chosen / totals).astype(jnp.bfloat16).astype(jnp.float32)
    pairs = jnp.concatenate([groups.astype(jnp.float32), slots.astype(jnp.float32), gates], axis=1).T
    pairs = jnp.concatenate([pairs, jnp.zeros((2, tokens), jnp.float32)], axis=0)
    world, acts, facts = gather_world(d_out, act_rows, pairs, dp_count, node_count)
    world = world.reshape(dp_count, group_tokens, feat_local)
    near = lax.dynamic_index_in_dim(world, me_dp, 0, keepdims=False)
    expert = me_node.astype(jnp.float32)
    live = (facts[:, :, 0:2] == expert) & (facts[:, :, 2:4] >= 0)
    source = jnp.arange(node_count, dtype=jnp.float32)[None, :, None, None] * cap_rows
    where = jnp.sum(jnp.where(live, facts[:, :, 2:4] + source + 1.0, 0.0), axis=2) - 1.0
    where = where.reshape(dp_count, group_tokens).astype(jnp.int32)
    gate = jnp.sum(jnp.where(live, facts[:, :, 4:6], 0.0), axis=2).reshape(dp_count, group_tokens)

    own_where = lax.dynamic_index_in_dim(where, me_dp, 0, keepdims=False)
    own_gate = lax.dynamic_index_in_dim(gate, me_dp, 0, keepdims=False)
    fills = jnp.arange(slot_count, dtype=jnp.int32)[:, None] == own_where[None, :]
    rows = jnp.dot(
        fills.astype(jnp.bfloat16), near, preferred_element_type=jnp.float32
    ).astype(jnp.bfloat16)
    row_gate = jnp.sum(jnp.where(fills, own_gate[None, :], 0.0), axis=1)
    term = lax.dot_general(rows, weight, (((1,), (1,)), ((), ())), preferred_element_type=jnp.float32)
    dot_part = jnp.sum(act_rows.astype(jnp.float32) * term, axis=1)
    half = hid_units // 2
    gated = row_gate[:, None] * term
    away = lax.dynamic_slice_in_dim(gated, (1 - me_local) * half, half, axis=1).astype(jnp.bfloat16)
    home = lax.dynamic_slice_in_dim(gated, me_local * half, half, axis=1)
    come = lax.ppermute(away, "local", [(0, 1), (1, 0)])
    d_hidden = (home + come.astype(jnp.float32)).astype(jnp.bfloat16)
    d_hidden = d_hidden.reshape(1, 1, node_count, cap_rows, half)

    token_dot = jnp.sum(jnp.where(fills, dot_part[:, None], 0.0), axis=0)
    parts = token_dot.reshape(node_count, tokens)
    kept = lax.dynamic_slice_in_dim(parts, me_node, 1, axis=0)
    my_dots = jnp.where(jnp.arange(node_count)[:, None] == me_node, kept, 0.0)
    members = node_count * 2
    me = me_node * 2 + me_local
    for step in range(1, members):
        target, origin = lax.rem(me + step, members), lax.rem(me - step + members, members)
        sent = lax.dynamic_slice_in_dim(parts, target // 2, 1, axis=0)
        got = lax.ppermute(sent, ("node", "local"), [(i, (i + step) % members) for i in range(members)])
        my_dots = my_dots + jnp.where(jnp.arange(node_count)[:, None] == origin // 2, got, 0.0)

    spots = (where[:, :, None] == jnp.arange(slot_count, dtype=jnp.int32)).astype(jnp.bfloat16)
    spots = spots * gate.astype(jnp.bfloat16)[:, :, None]
    left = jnp.einsum("dtc,dch->dth", spots, acts, preferred_element_type=jnp.float32).astype(jnp.bfloat16)
    d_wdown = lax.dot_general(
        left.reshape(dp_count * group_tokens, -1), world.reshape(dp_count * group_tokens, feat_local),
        (((0,), (0,)), ((), ())), preferred_element_type=jnp.float32,
    ).astype(jnp.bfloat16)
    d_wdown = d_wdown.reshape((1,) + d_wdown.shape)

    my_dots = my_dots.T
    route_dot = jnp.sum(picked * my_dots[:, None, :], axis=-1)
    return (logit_grads(picked, chosen, totals, route_dot), d_hidden, d_wdown)


def logit_grads(picked, chosen, totals, route_dot):
    mean_dot = jnp.sum(chosen / totals * route_dot, axis=-1, keepdims=True)
    d_chosen = route_scale * (route_dot - mean_dot) / totals
    return jnp.sum(picked * (d_chosen * chosen * (1.0 - chosen))[..., None], axis=1)


def shards(d_out, logits, groups, slots, hidden_act, w_down):
    node_count = lax.axis_size("node")
    expert_count = logits.shape[1]
    cap_rows = hidden_act.shape[3]
    hid_units = hidden_act.shape[4]
    feat_local = d_out.shape[1]
    scores = jax.nn.sigmoid(logits)
    picked = (groups[..., None] == jnp.arange(expert_count, dtype=jnp.int32)).astype(jnp.float32)
    chosen = jnp.sum(picked * scores[:, None, :], axis=-1)
    totals = jnp.sum(chosen, axis=-1, keepdims=True)
    gates = (route_scale * chosen / totals).astype(jnp.bfloat16)
    target = jnp.where(slots >= 0, groups * cap_rows + slots, -1)
    placed = (target[..., None] == jnp.arange(expert_count * cap_rows, dtype=jnp.int32)).astype(
        jnp.float32
    )
    send_rows = jnp.einsum(
        "tkc,td->cd", placed.astype(jnp.bfloat16), d_out, preferred_element_type=jnp.float32
    )
    send_rows = send_rows.astype(jnp.bfloat16).reshape(expert_count, cap_rows, feat_local)
    send_gates = jnp.einsum(
        "tkc,tk->c", placed, gates.astype(jnp.float32), precision=lax.Precision.HIGHEST
    )
    send_gates = send_gates.astype(jnp.bfloat16).reshape(expert_count, cap_rows)
    recv_rows, recv_gates = (
        lax.all_to_all(send_rows, "node", split_axis=0, concat_axis=0, tiled=True),
        lax.all_to_all(send_gates, "node", split_axis=0, concat_axis=0, tiled=True),
    )
    rows = recv_rows.reshape(node_count * cap_rows, feat_local)
    row_gate = recv_gates.reshape(node_count * cap_rows).astype(jnp.float32)
    act_rows = hidden_act.reshape(node_count * cap_rows, hid_units)
    weight = w_down.reshape(hid_units, feat_local)
    expert_out = jnp.dot(act_rows, weight, preferred_element_type=jnp.float32)
    dot_part = jnp.sum(rows.astype(jnp.float32) * expert_out, axis=-1)
    term = lax.dot_general(
        weight, rows, (((1,), (1,)), ((), ())), preferred_element_type=jnp.float32
    )
    summed = lax.psum_scatter(
        (term * row_gate[None, :]).astype(jnp.bfloat16), "local", scatter_dimension=0, tiled=True
    ).astype(jnp.float32)
    d_hidden = summed.T.astype(jnp.bfloat16).reshape(1, 1, node_count, cap_rows, summed.shape[0])
    scaled = (row_gate[:, None] * rows.astype(jnp.float32)).astype(jnp.bfloat16)
    weight_term = lax.dot_general(
        act_rows, scaled, (((0,), (0,)), ((), ())), preferred_element_type=jnp.float32
    )
    weight_sum = lax.psum_scatter(
        weight_term.astype(jnp.bfloat16), "dp", scatter_dimension=0, tiled=True
    ).astype(jnp.float32)
    d_wdown = weight_sum.astype(jnp.bfloat16).reshape(1, weight_sum.shape[0], feat_local)
    outgoing = lax.psum(dot_part, "local")
    returned = lax.all_to_all(
        outgoing.reshape(node_count, cap_rows), "node", split_axis=0, concat_axis=0, tiled=True
    ).reshape(node_count * cap_rows)
    route_dot = jnp.einsum("tkc,c->tk", placed, returned, precision=lax.Precision.HIGHEST)
    shares = chosen / totals
    mean_dot = jnp.sum(shares * route_dot, axis=-1, keepdims=True)
    d_chosen = route_scale * (route_dot - mean_dot) / totals
    d_logits = jnp.einsum("tke,tk->te", picked, d_chosen * chosen * (1.0 - chosen))
    return (d_logits, d_hidden, d_wdown)


def solution(mesh):
    in_specs = (
        P(("dp", "node"), "local"),
        P(("dp", "node"), None),
        P(("dp", "node"), None),
        P(("dp", "node"), None),
        P("dp", "node", None, None, None),
        P("node", None, "local"),
    )
    out_specs = (
        P(("dp", "node"), None),
        P("dp", "node", None, None, "local"),
        P("node", "dp", "local"),
    )

    def run(d_out, *rest):
        gathered = d_out.shape[0] * d_out.shape[1] // mesh.shape["local"] * d_out.dtype.itemsize
        fits = gathered <= gather_limit and mesh.shape["local"] == 2 and rest[0].shape[1] == mesh.shape["node"]
        body = gather_shards if fits else shards
        return jax.shard_map(body, mesh=mesh, in_specs=in_specs, out_specs=out_specs, check_vma=False)(d_out, *rest)

    return run
```

```python
import functools

import jax
import jax.numpy as jnp
from jax import lax
from jax.experimental import pallas as pl
from jax.experimental.pallas import tpu as pltpu
from jax.sharding import PartitionSpec as P

route_scale = 2.5
gather_limit = 20 * 1024 * 1024
chunk_rows = 32
pass_lag = 3
term_tile_hids = 256


def peer(**where):
    return dict(device_id=where, device_id_type=pl.DeviceIdType.MESH)


def greet(peers):
    barrier = pltpu.get_barrier_semaphore()
    for where in peers:
        pl.semaphore_signal(barrier, inc=1, **where)
    pl.semaphore_wait(barrier, len(peers))


def world_kernel(groups, nodes, own_ref, act_ref, facts_ref, w_ref, out_ref, act_out, facts_out, term_ref, stage, w_stage, local_sems,
                 z_recv, right_send, left_send, x_send, x_recv, c_send, c_recv, a_send, a_recv, f_send, f_recv):
    mine, node = lax.axis_index("dp"), lax.axis_index("node")
    chips = nodes // 2
    chip, core = node // 2, node % 2
    sibling = chip * 2 + 1 - core
    world = groups * nodes
    everyone = []
    for step in range(1, world):
        other = lax.rem(mine * nodes + node + step, world)
        everyone.append(peer(dp=other // nodes, node=other % nodes))
    greet(everyone)
    chunks = own_ref.shape[0] // chunk_rows
    part = act_out.shape[2]

    def block(source, origin, k):
        return out_ref.at[source, origin, pl.ds(k * chunk_rows, chunk_rows)]

    def own(k):
        return own_ref.at[pl.ds(k * chunk_rows, chunk_rows)]

    def hop(side, source, k, first):
        sems = right_send if side > 0 else left_send
        return pltpu.make_async_remote_copy(
            own(k) if first else block(source, node, k), block(source, node, k),
            sems.at[source, k], z_recv.at[source, k], **peer(dp=mine + side))

    def to_chip(source, step, k, first):
        return pltpu.make_async_remote_copy(
            own(k) if first else block(source, node, k), block(source, node, k),
            x_send.at[source, step - 1, k], x_recv.at[source, step - 1, k],
            **peer(node=lax.rem(chip + step, chips) * 2 + core))

    def to_core(source, step, k, first):
        origin = lax.rem(chip - step + chips, chips) * 2 + core
        return pltpu.make_async_remote_copy(
            own(k) if first and step == 0 else block(source, origin, k), block(source, origin, k),
            c_send.at[source, step, k], c_recv.at[source, step, k], **peer(node=sibling))

    def act_copy(step):
        target = lax.rem(mine + step, groups)
        columns = pl.ds(pl.multiple_of(target * part, part), part)
        return pltpu.make_async_remote_copy(
            act_ref.at[:, columns], act_out.at[mine], a_send.at[step - 1], a_recv.at[step - 1],
            **peer(dp=target))

    def fact_copy(step):
        return pltpu.make_async_remote_copy(
            facts_ref, facts_out.at[mine, node], f_send.at[step - 1], f_recv.at[step - 1], **everyone[step - 1])

    def sides(distance):
        return (
            (1, mine - distance, mine - distance >= 0, jnp.logical_and(mine - distance >= 0, mine + 1 < groups)),
            (-1, mine + distance, mine + distance < groups, jnp.logical_and(mine + distance < groups, mine > 0)),
        )

    def spread(distance, k):
        if distance == 0:
            for side, source, here, further in sides(0):
                @pl.when(further)
                def _():
                    hop(side, source, k, True).start()
            for step in range(1, chips):
                to_chip(mine, step, k, True).start()
            to_core(mine, 0, k, True).start()
            return
        for side, source, here, further in sides(distance):
            @pl.when(here)
            def _():
                hop(side, source, k, False).wait_recv()

            @pl.when(further)
            def _():
                hop(side, source, k, False).start()

            @pl.when(here)
            def _():
                for step in range(1, chips):
                    to_chip(source, step, k, False).start()
                to_core(source, 0, k, False).start()

    def pass_on(distance, k):
        for side, source, here, further in sides(distance)[:1 if distance == 0 else 2]:
            @pl.when(here)
            def _():
                for step in range(1, chips):
                    to_chip(source, step, k, distance == 0).wait_recv()
                    to_core(source, step, k, distance == 0).start()

    tokens = own_ref.shape[0]

    def staged(origin):
        return stage.at[pl.ds(pl.multiple_of(origin * tokens, tokens), tokens)]

    def near_copy(step):
        origin = lax.rem(node + step, nodes)
        return pltpu.make_async_copy(out_ref.at[mine, origin], staged(origin), local_sems.at[3 + step])

    def term_tile(tile):
        hids = pl.ds(tile * term_tile_hids, term_tile_hids)
        term_ref[:, hids] = lax.dot_general(
            stage[...], w_stage[hids, :], (((1,), (1,)), ((), ())), preferred_element_type=jnp.float32)

    fetch = pltpu.make_async_copy(own_ref, staged(node), local_sems.at[0])
    fetch.start()
    own_columns = pl.ds(pl.multiple_of(mine * part, part), part)
    keep_act = pltpu.make_async_copy(act_ref.at[:, own_columns], act_out.at[mine], local_sems.at[1])
    keep_act.start()
    keep_facts = pltpu.make_async_copy(facts_ref, facts_out.at[mine, node], local_sems.at[2])
    keep_facts.start()
    for k in range(chunks):
        spread(0, k)
    for step in range(1, groups):
        act_copy(step).start()
    for step in range(1, world):
        fact_copy(step).start()
    fetch.wait()
    keep = pltpu.make_async_copy(staged(node), out_ref.at[mine, node], local_sems.at[0])
    keep.start()
    w_copy = pltpu.make_async_copy(w_ref, w_stage, local_sems.at[3])
    w_copy.start()

    order = [(distance, k) for distance in range(groups) for k in range(chunks)]
    for at in range(chunks, len(order) + pass_lag):
        if at < len(order):
            spread(*order[at])
        if at == chunks:
            for item in order[:chunks - pass_lag]:
                pass_on(*item)
        pass_on(*order[at - pass_lag])
        if at == 2 * chunks:
            for k in range(chunks):
                for step in range(chips):
                    to_core(mine, step, k, True).wait_recv()
            for step in range(1, nodes):
                near_copy(step).start()
        if at == 2 * chunks + 1:
            for step in range(1, nodes):
                near_copy(step).wait()
            w_copy.wait()
        if at > 2 * chunks:
            tile = at - 2 * chunks - 1
            if tile < term_ref.shape[1] // term_tile_hids:
                term_tile(tile)

    for distance, k in order:
        for side, source, here, further in sides(distance):
            @pl.when(further)
            def _():
                hop(side, source, k, distance == 0).wait_send()

        for side, source, here, further in sides(distance)[:1 if distance == 0 else 2]:
            @pl.when(here)
            def _():
                for step in range(1, chips):
                    to_chip(source, step, k, distance == 0).wait_send()
                for step in range(chips):
                    to_core(source, step, k, distance == 0).wait_send()
                    if distance > 0:
                        to_core(source, step, k, False).wait_recv()
    for step in range(1, groups):
        act_copy(step).wait()
    for step in range(1, world):
        fact_copy(step).wait()
    keep.wait()
    keep_act.wait()
    keep_facts.wait()


def anywhere(count):
    return [pl.BlockSpec(memory_space=pl.ANY)] * count


def gather_world(d_out, act, facts, weight, groups, nodes):
    chunks, chips = d_out.shape[0] // chunk_rows, nodes // 2
    dma = pltpu.SemaphoreType.DMA
    return pl.pallas_call(
        functools.partial(world_kernel, groups, nodes),
        out_shape=(
            jax.ShapeDtypeStruct((groups, nodes) + d_out.shape, d_out.dtype),
            jax.ShapeDtypeStruct((groups, act.shape[0], act.shape[1] // groups), act.dtype),
            jax.ShapeDtypeStruct((groups, nodes) + facts.shape, facts.dtype),
            jax.ShapeDtypeStruct((nodes * d_out.shape[0], weight.shape[0]), jnp.float32),
        ),
        in_specs=anywhere(4),
        out_specs=tuple(anywhere(3)) + (pl.BlockSpec(memory_space=pltpu.VMEM),),
        scratch_shapes=[
            pltpu.VMEM((nodes * d_out.shape[0], d_out.shape[1]), d_out.dtype),
            pltpu.VMEM(weight.shape, weight.dtype),
            dma((3 + nodes,)), dma((groups, chunks)), dma((groups, chunks)), dma((groups, chunks)),
            dma((groups, chips - 1, chunks)), dma((groups, chips - 1, chunks)),
            dma((groups, chips, chunks)), dma((groups, chips, chunks)),
            dma((groups - 1,)), dma((groups - 1,)),
            dma((groups * nodes - 1,)), dma((groups * nodes - 1,)),
        ],
        cost_estimate=pl.CostEstimate(flops=0, bytes_accessed=200 << 20, transcendentals=0),
        compiler_params=pltpu.CompilerParams(collective_id=0, has_side_effects=True, vmem_limit_bytes=40 << 20),
    )(d_out, act, facts, weight)


def routing(logits, groups):
    scores = jax.nn.sigmoid(logits)
    picked = (groups[..., None] == jnp.arange(logits.shape[1], dtype=jnp.int32)).astype(jnp.float32)
    chosen = jnp.sum(picked * scores[:, None, :], axis=-1)
    totals = jnp.sum(chosen, axis=-1, keepdims=True)
    return picked, chosen, totals


def gather_shards(d_out, logits, groups, slots, hidden_act, w_down):
    dp_count, node_count = lax.axis_size("dp"), lax.axis_size("node")
    me_dp, me_node, me_local = lax.axis_index("dp"), lax.axis_index("node"), lax.axis_index("local")
    tokens, feat_local = d_out.shape
    cap_rows, hid_units = hidden_act.shape[3], hidden_act.shape[4]
    slot_count = node_count * cap_rows
    group_tokens = node_count * tokens
    act_rows = hidden_act.reshape(slot_count, hid_units)
    weight = w_down.reshape(hid_units, feat_local)

    picked, chosen, totals = routing(logits, groups)
    gates = (route_scale * chosen / totals).astype(jnp.bfloat16).astype(jnp.float32)
    pairs = jnp.concatenate([groups.astype(jnp.float32), slots.astype(jnp.float32), gates], axis=1).T
    pairs = jnp.concatenate([pairs, jnp.zeros((2, tokens), jnp.float32)], axis=0)
    world, acts, facts, term = gather_world(d_out, act_rows, pairs, weight, dp_count, node_count)
    expert = me_node.astype(jnp.float32)
    live = (facts[:, :, 0:2] == expert) & (facts[:, :, 2:4] >= 0)
    source = jnp.arange(node_count, dtype=jnp.float32)[None, :, None, None] * cap_rows
    where = jnp.sum(jnp.where(live, facts[:, :, 2:4] + source + 1.0, 0.0), axis=2) - 1.0
    where = where.reshape(dp_count, group_tokens).astype(jnp.int32)
    gate = jnp.sum(jnp.where(live, facts[:, :, 4:6], 0.0), axis=2).reshape(dp_count, group_tokens)

    own_where = lax.dynamic_index_in_dim(where, me_dp, 0, keepdims=False)
    own_gate = lax.dynamic_index_in_dim(gate, me_dp, 0, keepdims=False)
    fills = jnp.arange(slot_count, dtype=jnp.int32)[:, None] == own_where[None, :]
    fills = fills.astype(jnp.bfloat16)
    token_act = lax.dot_general(fills, act_rows, (((0,), (0,)), ((), ())), preferred_element_type=jnp.float32)
    token_dot = jnp.sum(token_act * term, axis=1)
    half = hid_units // 2
    gated = (own_gate[:, None] * term).astype(jnp.bfloat16)
    gated = jnp.dot(fills, gated, preferred_element_type=jnp.float32).astype(jnp.bfloat16)
    away = lax.dynamic_slice_in_dim(gated, (1 - me_local) * half, half, axis=1)
    home = lax.dynamic_slice_in_dim(gated, me_local * half, half, axis=1)
    away, token_dot, acts = lax.optimization_barrier((away, token_dot, acts))
    come = lax.ppermute(away, "local", [(0, 1), (1, 0)])
    d_hidden = (home.astype(jnp.float32) + come.astype(jnp.float32)).astype(jnp.bfloat16)
    d_hidden = d_hidden.reshape(1, 1, node_count, cap_rows, half)

    parts = token_dot.reshape(node_count, tokens)
    kept = lax.dynamic_slice_in_dim(parts, me_node, 1, axis=0)
    my_dots = jnp.where(jnp.arange(node_count)[:, None] == me_node, kept, 0.0)
    for step in range(1, node_count):
        target, origin = lax.rem(me_node + step, node_count), lax.rem(me_node - step + node_count, node_count)
        sent = lax.dynamic_slice_in_dim(parts, target, 1, axis=0)
        got = lax.ppermute(sent, "node", [(i, (i + step) % node_count) for i in range(node_count)])
        my_dots = my_dots + jnp.where(jnp.arange(node_count)[:, None] == origin, got, 0.0)
    my_dots = my_dots + lax.ppermute(my_dots, "local", [(0, 1), (1, 0)])

    spots = (where[:, :, None] == jnp.arange(slot_count, dtype=jnp.int32)).astype(jnp.bfloat16)
    spots = spots * gate.astype(jnp.bfloat16)[:, :, None]
    left = jnp.einsum("dtc,dch->dth", spots, acts, preferred_element_type=jnp.float32).astype(jnp.bfloat16)
    d_wdown = lax.dot_general(
        left.reshape(dp_count * group_tokens, -1), world.reshape(dp_count * group_tokens, feat_local),
        (((0,), (0,)), ((), ())), preferred_element_type=jnp.float32,
    ).astype(jnp.bfloat16)
    d_wdown = d_wdown.reshape((1,) + d_wdown.shape)

    my_dots = my_dots.T
    route_dot = jnp.sum(picked * my_dots[:, None, :], axis=-1)
    return (logit_grads(picked, chosen, totals, route_dot), d_hidden, d_wdown)


def logit_grads(picked, chosen, totals, route_dot):
    mean_dot = jnp.sum(chosen / totals * route_dot, axis=-1, keepdims=True)
    d_chosen = route_scale * (route_dot - mean_dot) / totals
    return jnp.sum(picked * (d_chosen * chosen * (1.0 - chosen))[..., None], axis=1)


def shards(d_out, logits, groups, slots, hidden_act, w_down):
    node_count = lax.axis_size("node")
    expert_count = logits.shape[1]
    cap_rows = hidden_act.shape[3]
    hid_units = hidden_act.shape[4]
    feat_local = d_out.shape[1]
    scores = jax.nn.sigmoid(logits)
    picked = (groups[..., None] == jnp.arange(expert_count, dtype=jnp.int32)).astype(jnp.float32)
    chosen = jnp.sum(picked * scores[:, None, :], axis=-1)
    totals = jnp.sum(chosen, axis=-1, keepdims=True)
    gates = (route_scale * chosen / totals).astype(jnp.bfloat16)
    target = jnp.where(slots >= 0, groups * cap_rows + slots, -1)
    placed = (target[..., None] == jnp.arange(expert_count * cap_rows, dtype=jnp.int32)).astype(
        jnp.float32
    )
    send_rows = jnp.einsum(
        "tkc,td->cd", placed.astype(jnp.bfloat16), d_out, preferred_element_type=jnp.float32
    )
    send_rows = send_rows.astype(jnp.bfloat16).reshape(expert_count, cap_rows, feat_local)
    send_gates = jnp.einsum(
        "tkc,tk->c", placed, gates.astype(jnp.float32), precision=lax.Precision.HIGHEST
    )
    send_gates = send_gates.astype(jnp.bfloat16).reshape(expert_count, cap_rows)
    recv_rows, recv_gates = (
        lax.all_to_all(send_rows, "node", split_axis=0, concat_axis=0, tiled=True),
        lax.all_to_all(send_gates, "node", split_axis=0, concat_axis=0, tiled=True),
    )
    rows = recv_rows.reshape(node_count * cap_rows, feat_local)
    row_gate = recv_gates.reshape(node_count * cap_rows).astype(jnp.float32)
    act_rows = hidden_act.reshape(node_count * cap_rows, hid_units)
    weight = w_down.reshape(hid_units, feat_local)
    expert_out = jnp.dot(act_rows, weight, preferred_element_type=jnp.float32)
    dot_part = jnp.sum(rows.astype(jnp.float32) * expert_out, axis=-1)
    term = lax.dot_general(
        weight, rows, (((1,), (1,)), ((), ())), preferred_element_type=jnp.float32
    )
    summed = lax.psum_scatter(
        (term * row_gate[None, :]).astype(jnp.bfloat16), "local", scatter_dimension=0, tiled=True
    ).astype(jnp.float32)
    d_hidden = summed.T.astype(jnp.bfloat16).reshape(1, 1, node_count, cap_rows, summed.shape[0])
    scaled = (row_gate[:, None] * rows.astype(jnp.float32)).astype(jnp.bfloat16)
    weight_term = lax.dot_general(
        act_rows, scaled, (((0,), (0,)), ((), ())), preferred_element_type=jnp.float32
    )
    weight_sum = lax.psum_scatter(
        weight_term.astype(jnp.bfloat16), "dp", scatter_dimension=0, tiled=True
    ).astype(jnp.float32)
    d_wdown = weight_sum.astype(jnp.bfloat16).reshape(1, weight_sum.shape[0], feat_local)
    outgoing = lax.psum(dot_part, "local")
    returned = lax.all_to_all(
        outgoing.reshape(node_count, cap_rows), "node", split_axis=0, concat_axis=0, tiled=True
    ).reshape(node_count * cap_rows)
    route_dot = jnp.einsum("tkc,c->tk", placed, returned, precision=lax.Precision.HIGHEST)
    shares = chosen / totals
    mean_dot = jnp.sum(shares * route_dot, axis=-1, keepdims=True)
    d_chosen = route_scale * (route_dot - mean_dot) / totals
    d_logits = jnp.einsum("tke,tk->te", picked, d_chosen * chosen * (1.0 - chosen))
    return (d_logits, d_hidden, d_wdown)


def solution(mesh):
    in_specs = (
        P(("dp", "node"), "local"),
        P(("dp", "node"), None),
        P(("dp", "node"), None),
        P(("dp", "node"), None),
        P("dp", "node", None, None, None),
        P("node", None, "local"),
    )
    out_specs = (
        P(("dp", "node"), None),
        P("dp", "node", None, None, "local"),
        P("node", "dp", "local"),
    )

    def run(d_out, *rest):
        gathered = d_out.shape[0] * d_out.shape[1] // mesh.shape["local"] * d_out.dtype.itemsize
        fits = gathered <= gather_limit and mesh.shape["local"] == 2 and rest[0].shape[1] == mesh.shape["node"]
        body = gather_shards if fits else shards
        return jax.shard_map(body, mesh=mesh, in_specs=in_specs, out_specs=out_specs, check_vma=False)(d_out, *rest)

    return run
```

```python
import functools

import jax
import jax.numpy as jnp
from jax import lax
from jax.experimental import pallas as pl
from jax.experimental.pallas import tpu as pltpu
from jax.sharding import PartitionSpec as P

route_scale = 2.5
gather_limit = 20 * 1024 * 1024
chunk_rows = 32
pass_lag = 3
term_tile_hids = 256


def peer(**where):
    return dict(device_id=where, device_id_type=pl.DeviceIdType.MESH)


def greet(peers):
    barrier = pltpu.get_barrier_semaphore()
    for where in peers:
        pl.semaphore_signal(barrier, inc=1, **where)
    pl.semaphore_wait(barrier, len(peers))


def world_kernel(groups, nodes, own_ref, act_ref, facts_ref, w_ref, out_ref, act_out, facts_out, term_ref, stage, w_stage, local_sems,
                 z_recv, right_send, left_send, x_send, x_recv, c_send, c_recv, a_send, a_recv, f_send, f_recv, cross_send):
    mine, node = lax.axis_index("dp"), lax.axis_index("node")
    chips = nodes // 2
    chip, core = node // 2, node % 2
    sibling = chip * 2 + 1 - core
    world = groups * nodes
    everyone = []
    for step in range(1, world):
        other = lax.rem(mine * nodes + node + step, world)
        everyone.append(peer(dp=other // nodes, node=other % nodes))
    greet(everyone)
    chunks = own_ref.shape[0] // chunk_rows
    part = act_out.shape[2]

    def block(source, origin, k):
        return out_ref.at[source, origin, pl.ds(k * chunk_rows, chunk_rows)]

    def own(k):
        return own_ref.at[pl.ds(k * chunk_rows, chunk_rows)]

    def hop(side, source, k, first):
        sems = right_send if side > 0 else left_send
        return pltpu.make_async_remote_copy(
            own(k) if first else block(source, node, k), block(source, node, k),
            sems.at[source, k], z_recv.at[source, k], **peer(dp=mine + side))

    def to_chip(source, step, k, first):
        return pltpu.make_async_remote_copy(
            own(k) if first else block(source, node, k), block(source, node, k),
            x_send.at[source, step - 1, k], x_recv.at[source, step - 1, k],
            **peer(node=lax.rem(chip + step, chips) * 2 + core))

    def to_core(source, step, k, first):
        origin = lax.rem(chip - step + chips, chips) * 2 + core
        return pltpu.make_async_remote_copy(
            own(k) if first and step == 0 else block(source, origin, k), block(source, origin, k),
            c_send.at[source, step, k], c_recv.at[source, step, k], **peer(node=sibling))

    def crossed(distance, k):
        return distance == 1 and k == chunks - 1

    def cross(side, step):
        origin = lax.rem(chip - step + chips, chips) * 2 + core
        held = block(mine, origin, chunks - 1)
        return pltpu.make_async_remote_copy(
            held, held, cross_send.at[(1 - side) // 2, step - 1], x_recv.at[mine, step - 1, chunks - 1],
            **peer(dp=mine + side))

    def act_copy(step):
        target = lax.rem(mine + step, groups)
        columns = pl.ds(pl.multiple_of(target * part, part), part)
        return pltpu.make_async_remote_copy(
            act_ref.at[:, columns], act_out.at[mine], a_send.at[step - 1], a_recv.at[step - 1],
            **peer(dp=target))

    def fact_copy(step):
        return pltpu.make_async_remote_copy(
            facts_ref, facts_out.at[mine, node], f_send.at[step - 1], f_recv.at[step - 1], **everyone[step - 1])

    def sides(distance):
        return (
            (1, mine - distance, mine - distance >= 0, jnp.logical_and(mine - distance >= 0, mine + 1 < groups)),
            (-1, mine + distance, mine + distance < groups, jnp.logical_and(mine + distance < groups, mine > 0)),
        )

    def spread(distance, k):
        if distance == 0:
            for side, source, here, further in sides(0):
                @pl.when(further)
                def _():
                    hop(side, source, k, True).start()
            for step in range(1, chips):
                to_chip(mine, step, k, True).start()
            to_core(mine, 0, k, True).start()
            return
        for side, source, here, further in sides(distance):
            @pl.when(here)
            def _():
                hop(side, source, k, False).wait_recv()

            @pl.when(further)
            def _():
                hop(side, source, k, False).start()

            @pl.when(here)
            def _():
                if not crossed(distance, k):
                    for step in range(1, chips):
                        to_chip(source, step, k, False).start()
                to_core(source, 0, k, False).start()

    def pass_on(distance, k):
        for side, source, here, further in sides(distance)[:1 if distance == 0 else 2]:
            @pl.when(here)
            def _():
                for step in range(1, chips):
                    to_chip(source, step, k, distance == 0).wait_recv()
                    to_core(source, step, k, distance == 0).start()
        if distance == 0 and k == chunks - 1:
            for side, source, here, further in sides(0):
                @pl.when(further)
                def _():
                    for step in range(1, chips):
                        cross(side, step).start()

    tokens = own_ref.shape[0]

    def staged(origin):
        return stage.at[pl.ds(pl.multiple_of(origin * tokens, tokens), tokens)]

    def near_copy(step):
        origin = lax.rem(node + step, nodes)
        return pltpu.make_async_copy(out_ref.at[mine, origin], staged(origin), local_sems.at[3 + step])

    def term_tile(tile):
        hids = pl.ds(tile * term_tile_hids, term_tile_hids)
        term_ref[:, hids] = lax.dot_general(
            stage[...], w_stage[hids, :], (((1,), (1,)), ((), ())), preferred_element_type=jnp.float32)

    fetch = pltpu.make_async_copy(own_ref, staged(node), local_sems.at[0])
    fetch.start()
    own_columns = pl.ds(pl.multiple_of(mine * part, part), part)
    keep_act = pltpu.make_async_copy(act_ref.at[:, own_columns], act_out.at[mine], local_sems.at[1])
    keep_act.start()
    keep_facts = pltpu.make_async_copy(facts_ref, facts_out.at[mine, node], local_sems.at[2])
    keep_facts.start()
    for k in range(chunks):
        spread(0, k)
    for step in range(1, groups):
        act_copy(step).start()
    for step in range(1, world):
        fact_copy(step).start()
    fetch.wait()
    keep = pltpu.make_async_copy(staged(node), out_ref.at[mine, node], local_sems.at[0])
    keep.start()
    w_copy = pltpu.make_async_copy(w_ref, w_stage, local_sems.at[3])
    w_copy.start()

    order = [(distance, k) for distance in range(groups) for k in range(chunks)]
    for at in range(chunks, len(order) + pass_lag):
        if at < len(order):
            spread(*order[at])
        if at == chunks:
            for item in order[:chunks - pass_lag]:
                pass_on(*item)
        pass_on(*order[at - pass_lag])
        if at == 2 * chunks:
            for k in range(chunks):
                for step in range(chips):
                    to_core(mine, step, k, True).wait_recv()
            for step in range(1, nodes):
                near_copy(step).start()
        if at == 2 * chunks + 1:
            for step in range(1, nodes):
                near_copy(step).wait()
            w_copy.wait()
        if at > 2 * chunks:
            tile = at - 2 * chunks - 1
            if tile < term_ref.shape[1] // term_tile_hids:
                term_tile(tile)

    for distance, k in order:
        for side, source, here, further in sides(distance):
            @pl.when(further)
            def _():
                hop(side, source, k, distance == 0).wait_send()

        for side, source, here, further in sides(distance)[:1 if distance == 0 else 2]:
            @pl.when(here)
            def _():
                if not crossed(distance, k):
                    for step in range(1, chips):
                        to_chip(source, step, k, distance == 0).wait_send()
                for step in range(chips):
                    to_core(source, step, k, distance == 0).wait_send()
                    if distance > 0:
                        to_core(source, step, k, False).wait_recv()
    for side, source, here, further in sides(0):
        @pl.when(further)
        def _():
            for step in range(1, chips):
                cross(side, step).wait_send()
    for step in range(1, groups):
        act_copy(step).wait()
    for step in range(1, world):
        fact_copy(step).wait()
    keep.wait()
    keep_act.wait()
    keep_facts.wait()


def anywhere(count):
    return [pl.BlockSpec(memory_space=pl.ANY)] * count


def gather_world(d_out, act, facts, weight, groups, nodes):
    chunks, chips = d_out.shape[0] // chunk_rows, nodes // 2
    dma = pltpu.SemaphoreType.DMA
    return pl.pallas_call(
        functools.partial(world_kernel, groups, nodes),
        out_shape=(
            jax.ShapeDtypeStruct((groups, nodes) + d_out.shape, d_out.dtype),
            jax.ShapeDtypeStruct((groups, act.shape[0], act.shape[1] // groups), act.dtype),
            jax.ShapeDtypeStruct((groups, nodes) + facts.shape, facts.dtype),
            jax.ShapeDtypeStruct((nodes * d_out.shape[0], weight.shape[0]), jnp.float32),
        ),
        in_specs=anywhere(4),
        out_specs=tuple(anywhere(3)) + (pl.BlockSpec(memory_space=pltpu.VMEM),),
        scratch_shapes=[
            pltpu.VMEM((nodes * d_out.shape[0], d_out.shape[1]), d_out.dtype),
            pltpu.VMEM(weight.shape, weight.dtype),
            dma((3 + nodes,)), dma((groups, chunks)), dma((groups, chunks)), dma((groups, chunks)),
            dma((groups, chips - 1, chunks)), dma((groups, chips - 1, chunks)),
            dma((groups, chips, chunks)), dma((groups, chips, chunks)),
            dma((groups - 1,)), dma((groups - 1,)),
            dma((groups * nodes - 1,)), dma((groups * nodes - 1,)), dma((2, chips - 1)),
        ],
        cost_estimate=pl.CostEstimate(flops=0, bytes_accessed=200 << 20, transcendentals=0),
        compiler_params=pltpu.CompilerParams(collective_id=0, has_side_effects=True, vmem_limit_bytes=60 << 20),
    )(d_out, act, facts, weight)


def routing(logits, groups):
    scores = jax.nn.sigmoid(logits)
    picked = (groups[..., None] == jnp.arange(logits.shape[1], dtype=jnp.int32)).astype(jnp.float32)
    chosen = jnp.sum(picked * scores[:, None, :], axis=-1)
    totals = jnp.sum(chosen, axis=-1, keepdims=True)
    return picked, chosen, totals


def gather_shards(d_out, logits, groups, slots, hidden_act, w_down):
    dp_count, node_count = lax.axis_size("dp"), lax.axis_size("node")
    me_dp, me_node, me_local = lax.axis_index("dp"), lax.axis_index("node"), lax.axis_index("local")
    tokens, feat_local = d_out.shape
    cap_rows, hid_units = hidden_act.shape[3], hidden_act.shape[4]
    slot_count = node_count * cap_rows
    group_tokens = node_count * tokens
    act_rows = hidden_act.reshape(slot_count, hid_units)
    weight = w_down.reshape(hid_units, feat_local)

    picked, chosen, totals = routing(logits, groups)
    gates = (route_scale * chosen / totals).astype(jnp.bfloat16).astype(jnp.float32)
    pairs = jnp.concatenate([groups.astype(jnp.float32), slots.astype(jnp.float32), gates], axis=1).T
    pairs = jnp.concatenate([pairs, jnp.zeros((2, tokens), jnp.float32)], axis=0)
    world, acts, facts, term = gather_world(d_out, act_rows, pairs, weight, dp_count, node_count)
    expert = me_node.astype(jnp.float32)
    live = (facts[:, :, 0:2] == expert) & (facts[:, :, 2:4] >= 0)
    source = jnp.arange(node_count, dtype=jnp.float32)[None, :, None, None] * cap_rows
    where = jnp.sum(jnp.where(live, facts[:, :, 2:4] + source + 1.0, 0.0), axis=2) - 1.0
    where = where.reshape(dp_count, group_tokens).astype(jnp.int32)
    gate = jnp.sum(jnp.where(live, facts[:, :, 4:6], 0.0), axis=2).reshape(dp_count, group_tokens)

    own_where = lax.dynamic_index_in_dim(where, me_dp, 0, keepdims=False)
    own_gate = lax.dynamic_index_in_dim(gate, me_dp, 0, keepdims=False)
    fills = jnp.arange(slot_count, dtype=jnp.int32)[:, None] == own_where[None, :]
    fills = fills.astype(jnp.bfloat16)
    token_act = lax.dot_general(fills, act_rows, (((0,), (0,)), ((), ())), preferred_element_type=jnp.float32)
    token_dot = jnp.sum(token_act * term, axis=1)
    half = hid_units // 2
    gated = (own_gate[:, None] * term).astype(jnp.bfloat16)
    gated = jnp.dot(fills, gated, preferred_element_type=jnp.float32).astype(jnp.bfloat16)
    away = lax.dynamic_slice_in_dim(gated, (1 - me_local) * half, half, axis=1)
    home = lax.dynamic_slice_in_dim(gated, me_local * half, half, axis=1)
    away, token_dot, acts = lax.optimization_barrier((away, token_dot, acts))
    come = lax.ppermute(away, "local", [(0, 1), (1, 0)])
    d_hidden = (home.astype(jnp.float32) + come.astype(jnp.float32)).astype(jnp.bfloat16)
    d_hidden = d_hidden.reshape(1, 1, node_count, cap_rows, half)

    parts = token_dot.reshape(node_count, tokens)
    kept = lax.dynamic_slice_in_dim(parts, me_node, 1, axis=0)
    my_dots = jnp.where(jnp.arange(node_count)[:, None] == me_node, kept, 0.0)
    for step in range(1, node_count):
        target, origin = lax.rem(me_node + step, node_count), lax.rem(me_node - step + node_count, node_count)
        sent = lax.dynamic_slice_in_dim(parts, target, 1, axis=0)
        got = lax.ppermute(sent, "node", [(i, (i + step) % node_count) for i in range(node_count)])
        my_dots = my_dots + jnp.where(jnp.arange(node_count)[:, None] == origin, got, 0.0)
    my_dots = my_dots + lax.ppermute(my_dots, "local", [(0, 1), (1, 0)])

    spots = (where[:, :, None] == jnp.arange(slot_count, dtype=jnp.int32)).astype(jnp.bfloat16)
    spots = spots * gate.astype(jnp.bfloat16)[:, :, None]
    left = jnp.einsum("dtc,dch->dth", spots, acts, preferred_element_type=jnp.float32).astype(jnp.bfloat16)
    d_wdown = lax.dot_general(
        left.reshape(dp_count * group_tokens, -1), world.reshape(dp_count * group_tokens, feat_local),
        (((0,), (0,)), ((), ())), preferred_element_type=jnp.float32,
    ).astype(jnp.bfloat16)
    d_wdown = d_wdown.reshape((1,) + d_wdown.shape)

    my_dots = my_dots.T
    route_dot = jnp.sum(picked * my_dots[:, None, :], axis=-1)
    return (logit_grads(picked, chosen, totals, route_dot), d_hidden, d_wdown)


def logit_grads(picked, chosen, totals, route_dot):
    mean_dot = jnp.sum(chosen / totals * route_dot, axis=-1, keepdims=True)
    d_chosen = route_scale * (route_dot - mean_dot) / totals
    return jnp.sum(picked * (d_chosen * chosen * (1.0 - chosen))[..., None], axis=1)


def shards(d_out, logits, groups, slots, hidden_act, w_down):
    node_count = lax.axis_size("node")
    expert_count = logits.shape[1]
    cap_rows = hidden_act.shape[3]
    hid_units = hidden_act.shape[4]
    feat_local = d_out.shape[1]
    scores = jax.nn.sigmoid(logits)
    picked = (groups[..., None] == jnp.arange(expert_count, dtype=jnp.int32)).astype(jnp.float32)
    chosen = jnp.sum(picked * scores[:, None, :], axis=-1)
    totals = jnp.sum(chosen, axis=-1, keepdims=True)
    gates = (route_scale * chosen / totals).astype(jnp.bfloat16)
    target = jnp.where(slots >= 0, groups * cap_rows + slots, -1)
    placed = (target[..., None] == jnp.arange(expert_count * cap_rows, dtype=jnp.int32)).astype(
        jnp.float32
    )
    send_rows = jnp.einsum(
        "tkc,td->cd", placed.astype(jnp.bfloat16), d_out, preferred_element_type=jnp.float32
    )
    send_rows = send_rows.astype(jnp.bfloat16).reshape(expert_count, cap_rows, feat_local)
    send_gates = jnp.einsum(
        "tkc,tk->c", placed, gates.astype(jnp.float32), precision=lax.Precision.HIGHEST
    )
    send_gates = send_gates.astype(jnp.bfloat16).reshape(expert_count, cap_rows)
    recv_rows, recv_gates = (
        lax.all_to_all(send_rows, "node", split_axis=0, concat_axis=0, tiled=True),
        lax.all_to_all(send_gates, "node", split_axis=0, concat_axis=0, tiled=True),
    )
    rows = recv_rows.reshape(node_count * cap_rows, feat_local)
    row_gate = recv_gates.reshape(node_count * cap_rows).astype(jnp.float32)
    act_rows = hidden_act.reshape(node_count * cap_rows, hid_units)
    weight = w_down.reshape(hid_units, feat_local)
    expert_out = jnp.dot(act_rows, weight, preferred_element_type=jnp.float32)
    dot_part = jnp.sum(rows.astype(jnp.float32) * expert_out, axis=-1)
    term = lax.dot_general(
        weight, rows, (((1,), (1,)), ((), ())), preferred_element_type=jnp.float32
    )
    summed = lax.psum_scatter(
        (term * row_gate[None, :]).astype(jnp.bfloat16), "local", scatter_dimension=0, tiled=True
    ).astype(jnp.float32)
    d_hidden = summed.T.astype(jnp.bfloat16).reshape(1, 1, node_count, cap_rows, summed.shape[0])
    scaled = (row_gate[:, None] * rows.astype(jnp.float32)).astype(jnp.bfloat16)
    weight_term = lax.dot_general(
        act_rows, scaled, (((0,), (0,)), ((), ())), preferred_element_type=jnp.float32
    )
    weight_sum = lax.psum_scatter(
        weight_term.astype(jnp.bfloat16), "dp", scatter_dimension=0, tiled=True
    ).astype(jnp.float32)
    d_wdown = weight_sum.astype(jnp.bfloat16).reshape(1, weight_sum.shape[0], feat_local)
    outgoing = lax.psum(dot_part, "local")
    returned = lax.all_to_all(
        outgoing.reshape(node_count, cap_rows), "node", split_axis=0, concat_axis=0, tiled=True
    ).reshape(node_count * cap_rows)
    route_dot = jnp.einsum("tkc,c->tk", placed, returned, precision=lax.Precision.HIGHEST)
    shares = chosen / totals
    mean_dot = jnp.sum(shares * route_dot, axis=-1, keepdims=True)
    d_chosen = route_scale * (route_dot - mean_dot) / totals
    d_logits = jnp.einsum("tke,tk->te", picked, d_chosen * chosen * (1.0 - chosen))
    return (d_logits, d_hidden, d_wdown)


def solution(mesh):
    in_specs = (
        P(("dp", "node"), "local"),
        P(("dp", "node"), None),
        P(("dp", "node"), None),
        P(("dp", "node"), None),
        P("dp", "node", None, None, None),
        P("node", None, "local"),
    )
    out_specs = (
        P(("dp", "node"), None),
        P("dp", "node", None, None, "local"),
        P("node", "dp", "local"),
    )

    def run(d_out, *rest):
        gathered = d_out.shape[0] * d_out.shape[1] // mesh.shape["local"] * d_out.dtype.itemsize
        fits = gathered <= gather_limit and mesh.shape["local"] == 2 and rest[0].shape[1] == mesh.shape["node"]
        body = gather_shards if fits else shards
        return jax.shard_map(body, mesh=mesh, in_specs=in_specs, out_specs=out_specs, check_vma=False)(d_out, *rest)

    return run
```

```python
import functools

import jax
import jax.numpy as jnp
from jax import lax
from jax.experimental import pallas as pl
from jax.experimental.pallas import tpu as pltpu
from jax.sharding import PartitionSpec as P

route_scale = 2.5
gather_limit = 20 * 1024 * 1024
chunk_rows = 32
pass_lag = 3
term_tile_hids = 256


def peer(**where):
    return dict(device_id=where, device_id_type=pl.DeviceIdType.MESH)


def greet(peers):
    barrier = pltpu.get_barrier_semaphore()
    for where in peers:
        pl.semaphore_signal(barrier, inc=1, **where)
    pl.semaphore_wait(barrier, len(peers))


def world_kernel(groups, nodes, own_ref, act_ref, facts_ref, w_ref, out_ref, act_out, facts_out, term_ref, stage, w_stage, local_sems,
                 z_recv, right_send, left_send, x_send, x_recv, c_send, c_recv, a_send, a_recv, f_send, f_recv):
    mine, node = lax.axis_index("dp"), lax.axis_index("node")
    chips = nodes // 2
    chip, core = node // 2, node % 2
    sibling = chip * 2 + 1 - core
    world = groups * nodes
    everyone = []
    for step in range(1, world):
        other = lax.rem(mine * nodes + node + step, world)
        everyone.append(peer(dp=other // nodes, node=other % nodes))
    greet(everyone)
    chunks = own_ref.shape[0] // chunk_rows
    part = act_out.shape[2]

    def block(source, origin, k):
        return out_ref.at[source, origin, pl.ds(k * chunk_rows, chunk_rows)]

    def own(k):
        return own_ref.at[pl.ds(k * chunk_rows, chunk_rows)]

    def hop(side, source, k, first):
        sems = right_send if side > 0 else left_send
        return pltpu.make_async_remote_copy(
            own(k) if first else block(source, node, k), block(source, node, k),
            sems.at[source, k], z_recv.at[source, k], **peer(dp=mine + side))

    def to_chip(source, step, k, first):
        return pltpu.make_async_remote_copy(
            own(k) if first else block(source, node, k), block(source, node, k),
            x_send.at[source, step - 1, k], x_recv.at[source, step - 1, k],
            **peer(node=lax.rem(chip + step, chips) * 2 + core))

    def to_core(source, step, k, first):
        origin = lax.rem(chip - step + chips, chips) * 2 + core
        return pltpu.make_async_remote_copy(
            own(k) if first and step == 0 else block(source, origin, k), block(source, origin, k),
            c_send.at[source, step, k], c_recv.at[source, step, k], **peer(node=sibling))

    def act_copy(step):
        target = lax.rem(mine + step, groups)
        columns = pl.ds(pl.multiple_of(target * part, part), part)
        return pltpu.make_async_remote_copy(
            act_ref.at[:, columns], act_out.at[mine], a_send.at[step - 1], a_recv.at[step - 1],
            **peer(dp=target))

    def fact_copy(step):
        return pltpu.make_async_remote_copy(
            facts_ref, facts_out.at[mine, node], f_send.at[step - 1], f_recv.at[step - 1], **everyone[step - 1])

    def sides(distance):
        return (
            (1, mine - distance, mine - distance >= 0, jnp.logical_and(mine - distance >= 0, mine + 1 < groups)),
            (-1, mine + distance, mine + distance < groups, jnp.logical_and(mine + distance < groups, mine > 0)),
        )

    def spread(distance, k):
        if distance == 0:
            for side, source, here, further in sides(0):
                @pl.when(further)
                def _():
                    hop(side, source, k, True).start()
            for step in range(1, chips):
                to_chip(mine, step, k, True).start()
            to_core(mine, 0, k, True).start()
            return
        for side, source, here, further in sides(distance):
            @pl.when(here)
            def _():
                hop(side, source, k, False).wait_recv()

            @pl.when(further)
            def _():
                hop(side, source, k, False).start()

            @pl.when(here)
            def _():
                for step in range(1, chips):
                    to_chip(source, step, k, False).start()
                to_core(source, 0, k, False).start()

    def pass_on(distance, k):
        for side, source, here, further in sides(distance)[:1 if distance == 0 else 2]:
            @pl.when(here)
            def _():
                for step in range(1, chips):
                    to_chip(source, step, k, distance == 0).wait_recv()
                    to_core(source, step, k, distance == 0).start()

    tokens = own_ref.shape[0]

    def staged(origin):
        return stage.at[pl.ds(pl.multiple_of(origin * tokens, tokens), tokens)]

    def near_copy(step):
        origin = lax.rem(node + step, nodes)
        return pltpu.make_async_copy(out_ref.at[mine, origin], staged(origin), local_sems.at[3 + step])

    def term_tile(tile):
        hids = pl.ds(tile * term_tile_hids, term_tile_hids)
        term_ref[:, hids] = lax.dot_general(
            stage[...], w_stage[hids, :], (((1,), (1,)), ((), ())), preferred_element_type=jnp.float32)

    fetch = pltpu.make_async_copy(own_ref, staged(node), local_sems.at[0])
    fetch.start()
    own_columns = pl.ds(pl.multiple_of(mine * part, part), part)
    keep_act = pltpu.make_async_copy(act_ref.at[:, own_columns], act_out.at[mine], local_sems.at[1])
    keep_act.start()
    keep_facts = pltpu.make_async_copy(facts_ref, facts_out.at[mine, node], local_sems.at[2])
    keep_facts.start()
    for k in range(chunks):
        spread(0, k)
    for step in range(1, groups):
        act_copy(step).start()
    for step in range(1, world):
        fact_copy(step).start()
    fetch.wait()
    keep = pltpu.make_async_copy(staged(node), out_ref.at[mine, node], local_sems.at[0])
    keep.start()
    w_copy = pltpu.make_async_copy(w_ref, w_stage, local_sems.at[3])
    w_copy.start()

    order = [(distance, k) for distance in range(groups) for k in range(chunks)]
    for at in range(chunks, len(order) + pass_lag):
        if at < len(order):
            spread(*order[at])
        if at == chunks:
            for item in order[:chunks - pass_lag]:
                pass_on(*item)
        pass_on(*order[at - pass_lag])
        if at == 2 * chunks:
            for k in range(chunks):
                for step in range(chips):
                    to_core(mine, step, k, True).wait_recv()
            for step in range(1, nodes):
                near_copy(step).start()
        if at == 2 * chunks + 1:
            for step in range(1, nodes):
                near_copy(step).wait()
            w_copy.wait()
        if at > 2 * chunks:
            tile = at - 2 * chunks - 1
            if tile < term_ref.shape[1] // term_tile_hids:
                term_tile(tile)

    for distance, k in order:
        for side, source, here, further in sides(distance):
            @pl.when(further)
            def _():
                hop(side, source, k, distance == 0).wait_send()

        for side, source, here, further in sides(distance)[:1 if distance == 0 else 2]:
            @pl.when(here)
            def _():
                for step in range(1, chips):
                    to_chip(source, step, k, distance == 0).wait_send()
                for step in range(chips):
                    to_core(source, step, k, distance == 0).wait_send()
                    if distance > 0:
                        to_core(source, step, k, False).wait_recv()
    for step in range(1, groups):
        act_copy(step).wait()
    for step in range(1, world):
        fact_copy(step).wait()
    keep.wait()
    keep_act.wait()
    keep_facts.wait()


def anywhere(count):
    return [pl.BlockSpec(memory_space=pl.ANY)] * count


def gather_world(d_out, act, facts, weight, groups, nodes):
    chunks, chips = d_out.shape[0] // chunk_rows, nodes // 2
    dma = pltpu.SemaphoreType.DMA
    return pl.pallas_call(
        functools.partial(world_kernel, groups, nodes),
        out_shape=(
            jax.ShapeDtypeStruct((groups, nodes) + d_out.shape, d_out.dtype),
            jax.ShapeDtypeStruct((groups, act.shape[0], act.shape[1] // groups), act.dtype),
            jax.ShapeDtypeStruct((groups, nodes) + facts.shape, facts.dtype),
            jax.ShapeDtypeStruct((nodes * d_out.shape[0], weight.shape[0]), jnp.float32),
        ),
        in_specs=anywhere(4),
        out_specs=tuple(anywhere(3)) + (pl.BlockSpec(memory_space=pltpu.VMEM),),
        scratch_shapes=[
            pltpu.VMEM((nodes * d_out.shape[0], d_out.shape[1]), d_out.dtype),
            pltpu.VMEM(weight.shape, weight.dtype),
            dma((3 + nodes,)), dma((groups, chunks)), dma((groups, chunks)), dma((groups, chunks)),
            dma((groups, chips - 1, chunks)), dma((groups, chips - 1, chunks)),
            dma((groups, chips, chunks)), dma((groups, chips, chunks)),
            dma((groups - 1,)), dma((groups - 1,)),
            dma((groups * nodes - 1,)), dma((groups * nodes - 1,)),
        ],
        cost_estimate=pl.CostEstimate(flops=0, bytes_accessed=200 << 20, transcendentals=0),
        compiler_params=pltpu.CompilerParams(collective_id=0, has_side_effects=True, vmem_limit_bytes=60 << 20),
    )(d_out, act, facts, weight)


def routing(logits, groups):
    scores = jax.nn.sigmoid(logits)
    picked = (groups[..., None] == jnp.arange(logits.shape[1], dtype=jnp.int32)).astype(jnp.float32)
    chosen = jnp.sum(picked * scores[:, None, :], axis=-1)
    totals = jnp.sum(chosen, axis=-1, keepdims=True)
    return picked, chosen, totals


def gather_shards(d_out, logits, groups, slots, hidden_act, w_down):
    dp_count, node_count = lax.axis_size("dp"), lax.axis_size("node")
    me_dp, me_node, me_local = lax.axis_index("dp"), lax.axis_index("node"), lax.axis_index("local")
    tokens, feat_local = d_out.shape
    cap_rows, hid_units = hidden_act.shape[3], hidden_act.shape[4]
    slot_count = node_count * cap_rows
    group_tokens = node_count * tokens
    act_rows = hidden_act.reshape(slot_count, hid_units)
    weight = w_down.reshape(hid_units, feat_local)

    picked, chosen, totals = routing(logits, groups)
    gates = (route_scale * chosen / totals).astype(jnp.bfloat16).astype(jnp.float32)
    pairs = jnp.concatenate([groups.astype(jnp.float32), slots.astype(jnp.float32), gates], axis=1).T
    pairs = jnp.concatenate([pairs, jnp.zeros((2, tokens), jnp.float32)], axis=0)
    world, acts, facts, term = gather_world(d_out, act_rows, pairs, weight, dp_count, node_count)
    expert = me_node.astype(jnp.float32)
    live = (facts[:, :, 0:2] == expert) & (facts[:, :, 2:4] >= 0)
    source = jnp.arange(node_count, dtype=jnp.float32)[None, :, None, None] * cap_rows
    where = jnp.sum(jnp.where(live, facts[:, :, 2:4] + source + 1.0, 0.0), axis=2) - 1.0
    where = where.reshape(dp_count, group_tokens).astype(jnp.int32)
    gate = jnp.sum(jnp.where(live, facts[:, :, 4:6], 0.0), axis=2).reshape(dp_count, group_tokens)

    own_where = lax.dynamic_index_in_dim(where, me_dp, 0, keepdims=False)
    own_gate = lax.dynamic_index_in_dim(gate, me_dp, 0, keepdims=False)
    fills = jnp.arange(slot_count, dtype=jnp.int32)[:, None] == own_where[None, :]
    fills = fills.astype(jnp.bfloat16)
    token_act = lax.dot_general(fills, act_rows, (((0,), (0,)), ((), ())), preferred_element_type=jnp.float32)
    token_dot = jnp.sum(token_act * term, axis=1)
    half = hid_units // 2
    gated = (own_gate[:, None] * term).astype(jnp.bfloat16)
    gated = jnp.dot(fills, gated, preferred_element_type=jnp.float32).astype(jnp.bfloat16)
    away = lax.dynamic_slice_in_dim(gated, (1 - me_local) * half, half, axis=1)
    home = lax.dynamic_slice_in_dim(gated, me_local * half, half, axis=1)
    away, token_dot, acts = lax.optimization_barrier((away, token_dot, acts))
    come = lax.ppermute(away, "local", [(0, 1), (1, 0)])
    d_hidden = (home.astype(jnp.float32) + come.astype(jnp.float32)).astype(jnp.bfloat16)
    d_hidden = d_hidden.reshape(1, 1, node_count, cap_rows, half)

    parts = token_dot.reshape(node_count, tokens)
    kept = lax.dynamic_slice_in_dim(parts, me_node, 1, axis=0)
    my_dots = jnp.where(jnp.arange(node_count)[:, None] == me_node, kept, 0.0)
    for step in range(1, node_count):
        target, origin = lax.rem(me_node + step, node_count), lax.rem(me_node - step + node_count, node_count)
        sent = lax.dynamic_slice_in_dim(parts, target, 1, axis=0)
        got = lax.ppermute(sent, "node", [(i, (i + step) % node_count) for i in range(node_count)])
        my_dots = my_dots + jnp.where(jnp.arange(node_count)[:, None] == origin, got, 0.0)
    my_dots = my_dots + lax.ppermute(my_dots, "local", [(0, 1), (1, 0)])

    spots = (where[:, :, None] == jnp.arange(slot_count, dtype=jnp.int32)).astype(jnp.bfloat16)
    spots = spots * gate.astype(jnp.bfloat16)[:, :, None]
    left = jnp.einsum("dtc,dch->dth", spots, acts, preferred_element_type=jnp.float32).astype(jnp.bfloat16)
    d_wdown = lax.dot_general(
        left.reshape(dp_count * group_tokens, -1), world.reshape(dp_count * group_tokens, feat_local),
        (((0,), (0,)), ((), ())), preferred_element_type=jnp.float32,
    ).astype(jnp.bfloat16)
    d_wdown = d_wdown.reshape((1,) + d_wdown.shape)

    my_dots = my_dots.T
    route_dot = jnp.sum(picked * my_dots[:, None, :], axis=-1)
    return (logit_grads(picked, chosen, totals, route_dot), d_hidden, d_wdown)


def logit_grads(picked, chosen, totals, route_dot):
    mean_dot = jnp.sum(chosen / totals * route_dot, axis=-1, keepdims=True)
    d_chosen = route_scale * (route_dot - mean_dot) / totals
    return jnp.sum(picked * (d_chosen * chosen * (1.0 - chosen))[..., None], axis=1)


def shards(d_out, logits, groups, slots, hidden_act, w_down):
    node_count = lax.axis_size("node")
    expert_count = logits.shape[1]
    cap_rows = hidden_act.shape[3]
    hid_units = hidden_act.shape[4]
    feat_local = d_out.shape[1]
    scores = jax.nn.sigmoid(logits)
    picked = (groups[..., None] == jnp.arange(expert_count, dtype=jnp.int32)).astype(jnp.float32)
    chosen = jnp.sum(picked * scores[:, None, :], axis=-1)
    totals = jnp.sum(chosen, axis=-1, keepdims=True)
    gates = (route_scale * chosen / totals).astype(jnp.bfloat16)
    target = jnp.where(slots >= 0, groups * cap_rows + slots, -1)
    placed = (target[..., None] == jnp.arange(expert_count * cap_rows, dtype=jnp.int32)).astype(
        jnp.float32
    )
    send_rows = jnp.einsum(
        "tkc,td->cd", placed.astype(jnp.bfloat16), d_out, preferred_element_type=jnp.float32
    )
    send_rows = send_rows.astype(jnp.bfloat16).reshape(expert_count, cap_rows, feat_local)
    send_gates = jnp.einsum(
        "tkc,tk->c", placed, gates.astype(jnp.float32), precision=lax.Precision.HIGHEST
    )
    send_gates = send_gates.astype(jnp.bfloat16).reshape(expert_count, cap_rows)
    recv_rows, recv_gates = (
        lax.all_to_all(send_rows, "node", split_axis=0, concat_axis=0, tiled=True),
        lax.all_to_all(send_gates, "node", split_axis=0, concat_axis=0, tiled=True),
    )
    rows = recv_rows.reshape(node_count * cap_rows, feat_local)
    row_gate = recv_gates.reshape(node_count * cap_rows).astype(jnp.float32)
    act_rows = hidden_act.reshape(node_count * cap_rows, hid_units)
    weight = w_down.reshape(hid_units, feat_local)
    expert_out = jnp.dot(act_rows, weight, preferred_element_type=jnp.float32)
    dot_part = jnp.sum(rows.astype(jnp.float32) * expert_out, axis=-1)
    term = lax.dot_general(
        weight, rows, (((1,), (1,)), ((), ())), preferred_element_type=jnp.float32
    )
    summed = lax.psum_scatter(
        (term * row_gate[None, :]).astype(jnp.bfloat16), "local", scatter_dimension=0, tiled=True
    ).astype(jnp.float32)
    d_hidden = summed.T.astype(jnp.bfloat16).reshape(1, 1, node_count, cap_rows, summed.shape[0])
    scaled = (row_gate[:, None] * rows.astype(jnp.float32)).astype(jnp.bfloat16)
    weight_term = lax.dot_general(
        act_rows, scaled, (((0,), (0,)), ((), ())), preferred_element_type=jnp.float32
    )
    weight_sum = lax.psum_scatter(
        weight_term.astype(jnp.bfloat16), "dp", scatter_dimension=0, tiled=True
    ).astype(jnp.float32)
    d_wdown = weight_sum.astype(jnp.bfloat16).reshape(1, weight_sum.shape[0], feat_local)
    outgoing = lax.psum(dot_part, "local")
    returned = lax.all_to_all(
        outgoing.reshape(node_count, cap_rows), "node", split_axis=0, concat_axis=0, tiled=True
    ).reshape(node_count * cap_rows)
    route_dot = jnp.einsum("tkc,c->tk", placed, returned, precision=lax.Precision.HIGHEST)
    shares = chosen / totals
    mean_dot = jnp.sum(shares * route_dot, axis=-1, keepdims=True)
    d_chosen = route_scale * (route_dot - mean_dot) / totals
    d_logits = jnp.einsum("tke,tk->te", picked, d_chosen * chosen * (1.0 - chosen))
    return (d_logits, d_hidden, d_wdown)


def solution(mesh):
    in_specs = (
        P(("dp", "node"), "local"),
        P(("dp", "node"), None),
        P(("dp", "node"), None),
        P(("dp", "node"), None),
        P("dp", "node", None, None, None),
        P("node", None, "local"),
    )
    out_specs = (
        P(("dp", "node"), None),
        P("dp", "node", None, None, "local"),
        P("node", "dp", "local"),
    )

    def run(d_out, *rest):
        gathered = d_out.shape[0] * d_out.shape[1] // mesh.shape["local"] * d_out.dtype.itemsize
        fits = gathered <= gather_limit and mesh.shape["local"] == 2 and rest[0].shape[1] == mesh.shape["node"]
        body = gather_shards if fits else shards
        return jax.shard_map(body, mesh=mesh, in_specs=in_specs, out_specs=out_specs, check_vma=False)(d_out, *rest)

    return run
```

```python
import functools

import jax
import jax.numpy as jnp
from jax import lax
from jax.experimental import pallas as pl
from jax.experimental.pallas import tpu as pltpu
from jax.sharding import PartitionSpec as P

route_scale = 2.5
gather_limit = 20 * 1024 * 1024
chunk_rows = 32
pass_lag = 3
term_tile_hids = 256


def peer(**where):
    return dict(device_id=where, device_id_type=pl.DeviceIdType.MESH)


def greet(peers):
    barrier = pltpu.get_barrier_semaphore()
    for where in peers:
        pl.semaphore_signal(barrier, inc=1, **where)
    pl.semaphore_wait(barrier, len(peers))


def world_kernel(groups, nodes, own_ref, act_ref, facts_ref, w_ref, out_ref, act_out, facts_out, term_ref, stage, w_stage, local_sems,
                 z_recv, right_send, left_send, x_send, x_recv, c_send, c_recv, a_send, a_recv, f_send, f_recv):
    mine, node = lax.axis_index("dp"), lax.axis_index("node")
    chips = nodes // 2
    chip, core = node // 2, node % 2
    sibling = chip * 2 + 1 - core
    world = groups * nodes
    everyone = []
    for step in range(1, world):
        other = lax.rem(mine * nodes + node + step, world)
        everyone.append(peer(dp=other // nodes, node=other % nodes))
    greet(everyone)
    chunks = own_ref.shape[0] // chunk_rows
    part = act_out.shape[2]

    def block(source, origin, k):
        return out_ref.at[source, origin, pl.ds(k * chunk_rows, chunk_rows)]

    def own(k):
        return own_ref.at[pl.ds(k * chunk_rows, chunk_rows)]

    def hop(side, source, k, first):
        sems = right_send if side > 0 else left_send
        return pltpu.make_async_remote_copy(
            own(k) if first else block(source, node, k), block(source, node, k),
            sems.at[source, k], z_recv.at[source, k], **peer(dp=mine + side))

    def to_chip(source, step, k, first):
        return pltpu.make_async_remote_copy(
            own(k) if first else block(source, node, k), block(source, node, k),
            x_send.at[source, step - 1, k], x_recv.at[source, step - 1, k],
            **peer(node=lax.rem(chip + step, chips) * 2 + core))

    def to_core(source, step, k, first):
        origin = lax.rem(chip - step + chips, chips) * 2 + core
        return pltpu.make_async_remote_copy(
            own(k) if first and step == 0 else block(source, origin, k), block(source, origin, k),
            c_send.at[source, step, k], c_recv.at[source, step, k], **peer(node=sibling))

    def act_copy(step):
        target = lax.rem(mine + step, groups)
        columns = pl.ds(pl.multiple_of(target * part, part), part)
        return pltpu.make_async_remote_copy(
            act_ref.at[:, columns], act_out.at[mine], a_send.at[step - 1], a_recv.at[step - 1],
            **peer(dp=target))

    def fact_copy(step):
        return pltpu.make_async_remote_copy(
            facts_ref, facts_out.at[mine, node], f_send.at[step - 1], f_recv.at[step - 1], **everyone[step - 1])

    def sides(distance):
        return (
            (1, mine - distance, mine - distance >= 0, jnp.logical_and(mine - distance >= 0, mine + 1 < groups)),
            (-1, mine + distance, mine + distance < groups, jnp.logical_and(mine + distance < groups, mine > 0)),
        )

    def spread(distance, k):
        if distance == 0:
            for side, source, here, further in sides(0):
                @pl.when(further)
                def _():
                    hop(side, source, k, True).start()
            for step in range(1, chips):
                to_chip(mine, step, k, True).start()
            to_core(mine, 0, k, True).start()
            return
        for side, source, here, further in sides(distance):
            @pl.when(here)
            def _():
                hop(side, source, k, False).wait_recv()

            @pl.when(further)
            def _():
                hop(side, source, k, False).start()

            @pl.when(here)
            def _():
                for step in range(1, chips):
                    to_chip(source, step, k, False).start()
                to_core(source, 0, k, False).start()

    def pass_on(distance, k):
        for side, source, here, further in sides(distance)[:1 if distance == 0 else 2]:
            @pl.when(here)
            def _():
                for step in range(1, chips):
                    to_chip(source, step, k, distance == 0).wait_recv()
                    to_core(source, step, k, distance == 0).start()

    tokens = own_ref.shape[0]

    def staged(origin):
        return stage.at[pl.ds(pl.multiple_of(origin * tokens, tokens), tokens)]

    def near_copy(step):
        origin = lax.rem(node + step, nodes)
        return pltpu.make_async_copy(out_ref.at[mine, origin], staged(origin), local_sems.at[3 + step])

    def term_tile(tile):
        hids = pl.ds(tile * term_tile_hids, term_tile_hids)
        term_ref[:, hids] = lax.dot_general(
            stage[...], w_stage[hids, :], (((1,), (1,)), ((), ())), preferred_element_type=jnp.float32)

    fetch = pltpu.make_async_copy(own_ref, staged(node), local_sems.at[0])
    fetch.start()
    own_columns = pl.ds(pl.multiple_of(mine * part, part), part)
    keep_act = pltpu.make_async_copy(act_ref.at[:, own_columns], act_out.at[mine], local_sems.at[1])
    keep_act.start()
    keep_facts = pltpu.make_async_copy(facts_ref, facts_out.at[mine, node], local_sems.at[2])
    keep_facts.start()
    for k in range(chunks):
        spread(0, k)
    for step in range(1, world):
        fact_copy(step).start()
    fetch.wait()
    keep = pltpu.make_async_copy(staged(node), out_ref.at[mine, node], local_sems.at[0])
    keep.start()
    w_copy = pltpu.make_async_copy(w_ref, w_stage, local_sems.at[3])
    w_copy.start()

    order = [(distance, k) for distance in range(groups) for k in range(chunks)]
    for at in range(chunks, len(order) + pass_lag):
        if at < len(order):
            spread(*order[at])
        if at == chunks:
            for item in order[:chunks - pass_lag]:
                pass_on(*item)
        pass_on(*order[at - pass_lag])
        if at == 2 * chunks:
            for step in range(1, groups):
                act_copy(step).start()
            for k in range(chunks):
                for step in range(chips):
                    to_core(mine, step, k, True).wait_recv()
            for step in range(1, nodes):
                near_copy(step).start()
        if at == 2 * chunks + 1:
            for step in range(1, nodes):
                near_copy(step).wait()
            w_copy.wait()
        if at > 2 * chunks:
            tile = at - 2 * chunks - 1
            if tile < term_ref.shape[1] // term_tile_hids:
                term_tile(tile)

    for distance, k in order:
        for side, source, here, further in sides(distance):
            @pl.when(further)
            def _():
                hop(side, source, k, distance == 0).wait_send()

        for side, source, here, further in sides(distance)[:1 if distance == 0 else 2]:
            @pl.when(here)
            def _():
                for step in range(1, chips):
                    to_chip(source, step, k, distance == 0).wait_send()
                for step in range(chips):
                    to_core(source, step, k, distance == 0).wait_send()
                    if distance > 0:
                        to_core(source, step, k, False).wait_recv()
    for step in range(1, groups):
        act_copy(step).wait()
    for step in range(1, world):
        fact_copy(step).wait()
    keep.wait()
    keep_act.wait()
    keep_facts.wait()


def anywhere(count):
    return [pl.BlockSpec(memory_space=pl.ANY)] * count


def gather_world(d_out, act, facts, weight, groups, nodes):
    chunks, chips = d_out.shape[0] // chunk_rows, nodes // 2
    dma = pltpu.SemaphoreType.DMA
    return pl.pallas_call(
        functools.partial(world_kernel, groups, nodes),
        out_shape=(
            jax.ShapeDtypeStruct((groups, nodes) + d_out.shape, d_out.dtype),
            jax.ShapeDtypeStruct((groups, act.shape[0], act.shape[1] // groups), act.dtype),
            jax.ShapeDtypeStruct((groups, nodes) + facts.shape, facts.dtype),
            jax.ShapeDtypeStruct((nodes * d_out.shape[0], weight.shape[0]), jnp.float32),
        ),
        in_specs=anywhere(4),
        out_specs=tuple(anywhere(3)) + (pl.BlockSpec(memory_space=pltpu.VMEM),),
        scratch_shapes=[
            pltpu.VMEM((nodes * d_out.shape[0], d_out.shape[1]), d_out.dtype),
            pltpu.VMEM(weight.shape, weight.dtype),
            dma((3 + nodes,)), dma((groups, chunks)), dma((groups, chunks)), dma((groups, chunks)),
            dma((groups, chips - 1, chunks)), dma((groups, chips - 1, chunks)),
            dma((groups, chips, chunks)), dma((groups, chips, chunks)),
            dma((groups - 1,)), dma((groups - 1,)),
            dma((groups * nodes - 1,)), dma((groups * nodes - 1,)),
        ],
        cost_estimate=pl.CostEstimate(flops=0, bytes_accessed=200 << 20, transcendentals=0),
        compiler_params=pltpu.CompilerParams(collective_id=0, has_side_effects=True, vmem_limit_bytes=60 << 20),
    )(d_out, act, facts, weight)


def routing(logits, groups):
    scores = jax.nn.sigmoid(logits)
    picked = (groups[..., None] == jnp.arange(logits.shape[1], dtype=jnp.int32)).astype(jnp.float32)
    chosen = jnp.sum(picked * scores[:, None, :], axis=-1)
    totals = jnp.sum(chosen, axis=-1, keepdims=True)
    return picked, chosen, totals


def gather_shards(d_out, logits, groups, slots, hidden_act, w_down):
    dp_count, node_count = lax.axis_size("dp"), lax.axis_size("node")
    me_dp, me_node, me_local = lax.axis_index("dp"), lax.axis_index("node"), lax.axis_index("local")
    tokens, feat_local = d_out.shape
    cap_rows, hid_units = hidden_act.shape[3], hidden_act.shape[4]
    slot_count = node_count * cap_rows
    group_tokens = node_count * tokens
    act_rows = hidden_act.reshape(slot_count, hid_units)
    weight = w_down.reshape(hid_units, feat_local)

    picked, chosen, totals = routing(logits, groups)
    gates = (route_scale * chosen / totals).astype(jnp.bfloat16).astype(jnp.float32)
    pairs = jnp.concatenate([groups.astype(jnp.float32), slots.astype(jnp.float32), gates], axis=1).T
    pairs = jnp.concatenate([pairs, jnp.zeros((2, tokens), jnp.float32)], axis=0)
    world, acts, facts, term = gather_world(d_out, act_rows, pairs, weight, dp_count, node_count)
    expert = me_node.astype(jnp.float32)
    live = (facts[:, :, 0:2] == expert) & (facts[:, :, 2:4] >= 0)
    source = jnp.arange(node_count, dtype=jnp.float32)[None, :, None, None] * cap_rows
    where = jnp.sum(jnp.where(live, facts[:, :, 2:4] + source + 1.0, 0.0), axis=2) - 1.0
    where = where.reshape(dp_count, group_tokens).astype(jnp.int32)
    gate = jnp.sum(jnp.where(live, facts[:, :, 4:6], 0.0), axis=2).reshape(dp_count, group_tokens)

    own_where = lax.dynamic_index_in_dim(where, me_dp, 0, keepdims=False)
    own_gate = lax.dynamic_index_in_dim(gate, me_dp, 0, keepdims=False)
    fills = jnp.arange(slot_count, dtype=jnp.int32)[:, None] == own_where[None, :]
    fills = fills.astype(jnp.bfloat16)
    token_act = lax.dot_general(fills, act_rows, (((0,), (0,)), ((), ())), preferred_element_type=jnp.float32)
    token_dot = jnp.sum(token_act * term, axis=1)
    half = hid_units // 2
    gated = (own_gate[:, None] * term).astype(jnp.bfloat16)
    gated = jnp.dot(fills, gated, preferred_element_type=jnp.float32).astype(jnp.bfloat16)
    away = lax.dynamic_slice_in_dim(gated, (1 - me_local) * half, half, axis=1)
    home = lax.dynamic_slice_in_dim(gated, me_local * half, half, axis=1)
    away, token_dot, acts = lax.optimization_barrier((away, token_dot, acts))
    come = lax.ppermute(away, "local", [(0, 1), (1, 0)])
    d_hidden = (home.astype(jnp.float32) + come.astype(jnp.float32)).astype(jnp.bfloat16)
    d_hidden = d_hidden.reshape(1, 1, node_count, cap_rows, half)

    parts = token_dot.reshape(node_count, tokens)
    kept = lax.dynamic_slice_in_dim(parts, me_node, 1, axis=0)
    my_dots = jnp.where(jnp.arange(node_count)[:, None] == me_node, kept, 0.0)
    for step in range(1, node_count):
        target, origin = lax.rem(me_node + step, node_count), lax.rem(me_node - step + node_count, node_count)
        sent = lax.dynamic_slice_in_dim(parts, target, 1, axis=0)
        got = lax.ppermute(sent, "node", [(i, (i + step) % node_count) for i in range(node_count)])
        my_dots = my_dots + jnp.where(jnp.arange(node_count)[:, None] == origin, got, 0.0)
    my_dots = my_dots + lax.ppermute(my_dots, "local", [(0, 1), (1, 0)])

    spots = (where[:, :, None] == jnp.arange(slot_count, dtype=jnp.int32)).astype(jnp.bfloat16)
    spots = spots * gate.astype(jnp.bfloat16)[:, :, None]
    left = jnp.einsum("dtc,dch->dth", spots, acts, preferred_element_type=jnp.float32).astype(jnp.bfloat16)
    d_wdown = lax.dot_general(
        left.reshape(dp_count * group_tokens, -1), world.reshape(dp_count * group_tokens, feat_local),
        (((0,), (0,)), ((), ())), preferred_element_type=jnp.float32,
    ).astype(jnp.bfloat16)
    d_wdown = d_wdown.reshape((1,) + d_wdown.shape)

    my_dots = my_dots.T
    route_dot = jnp.sum(picked * my_dots[:, None, :], axis=-1)
    return (logit_grads(picked, chosen, totals, route_dot), d_hidden, d_wdown)


def logit_grads(picked, chosen, totals, route_dot):
    mean_dot = jnp.sum(chosen / totals * route_dot, axis=-1, keepdims=True)
    d_chosen = route_scale * (route_dot - mean_dot) / totals
    return jnp.sum(picked * (d_chosen * chosen * (1.0 - chosen))[..., None], axis=1)


def shards(d_out, logits, groups, slots, hidden_act, w_down):
    node_count = lax.axis_size("node")
    expert_count = logits.shape[1]
    cap_rows = hidden_act.shape[3]
    hid_units = hidden_act.shape[4]
    feat_local = d_out.shape[1]
    scores = jax.nn.sigmoid(logits)
    picked = (groups[..., None] == jnp.arange(expert_count, dtype=jnp.int32)).astype(jnp.float32)
    chosen = jnp.sum(picked * scores[:, None, :], axis=-1)
    totals = jnp.sum(chosen, axis=-1, keepdims=True)
    gates = (route_scale * chosen / totals).astype(jnp.bfloat16)
    target = jnp.where(slots >= 0, groups * cap_rows + slots, -1)
    placed = (target[..., None] == jnp.arange(expert_count * cap_rows, dtype=jnp.int32)).astype(
        jnp.float32
    )
    send_rows = jnp.einsum(
        "tkc,td->cd", placed.astype(jnp.bfloat16), d_out, preferred_element_type=jnp.float32
    )
    send_rows = send_rows.astype(jnp.bfloat16).reshape(expert_count, cap_rows, feat_local)
    send_gates = jnp.einsum(
        "tkc,tk->c", placed, gates.astype(jnp.float32), precision=lax.Precision.HIGHEST
    )
    send_gates = send_gates.astype(jnp.bfloat16).reshape(expert_count, cap_rows)
    recv_rows, recv_gates = (
        lax.all_to_all(send_rows, "node", split_axis=0, concat_axis=0, tiled=True),
        lax.all_to_all(send_gates, "node", split_axis=0, concat_axis=0, tiled=True),
    )
    rows = recv_rows.reshape(node_count * cap_rows, feat_local)
    row_gate = recv_gates.reshape(node_count * cap_rows).astype(jnp.float32)
    act_rows = hidden_act.reshape(node_count * cap_rows, hid_units)
    weight = w_down.reshape(hid_units, feat_local)
    expert_out = jnp.dot(act_rows, weight, preferred_element_type=jnp.float32)
    dot_part = jnp.sum(rows.astype(jnp.float32) * expert_out, axis=-1)
    term = lax.dot_general(
        weight, rows, (((1,), (1,)), ((), ())), preferred_element_type=jnp.float32
    )
    summed = lax.psum_scatter(
        (term * row_gate[None, :]).astype(jnp.bfloat16), "local", scatter_dimension=0, tiled=True
    ).astype(jnp.float32)
    d_hidden = summed.T.astype(jnp.bfloat16).reshape(1, 1, node_count, cap_rows, summed.shape[0])
    scaled = (row_gate[:, None] * rows.astype(jnp.float32)).astype(jnp.bfloat16)
    weight_term = lax.dot_general(
        act_rows, scaled, (((0,), (0,)), ((), ())), preferred_element_type=jnp.float32
    )
    weight_sum = lax.psum_scatter(
        weight_term.astype(jnp.bfloat16), "dp", scatter_dimension=0, tiled=True
    ).astype(jnp.float32)
    d_wdown = weight_sum.astype(jnp.bfloat16).reshape(1, weight_sum.shape[0], feat_local)
    outgoing = lax.psum(dot_part, "local")
    returned = lax.all_to_all(
        outgoing.reshape(node_count, cap_rows), "node", split_axis=0, concat_axis=0, tiled=True
    ).reshape(node_count * cap_rows)
    route_dot = jnp.einsum("tkc,c->tk", placed, returned, precision=lax.Precision.HIGHEST)
    shares = chosen / totals
    mean_dot = jnp.sum(shares * route_dot, axis=-1, keepdims=True)
    d_chosen = route_scale * (route_dot - mean_dot) / totals
    d_logits = jnp.einsum("tke,tk->te", picked, d_chosen * chosen * (1.0 - chosen))
    return (d_logits, d_hidden, d_wdown)


def solution(mesh):
    in_specs = (
        P(("dp", "node"), "local"),
        P(("dp", "node"), None),
        P(("dp", "node"), None),
        P(("dp", "node"), None),
        P("dp", "node", None, None, None),
        P("node", None, "local"),
    )
    out_specs = (
        P(("dp", "node"), None),
        P("dp", "node", None, None, "local"),
        P("node", "dp", "local"),
    )

    def run(d_out, *rest):
        gathered = d_out.shape[0] * d_out.shape[1] // mesh.shape["local"] * d_out.dtype.itemsize
        fits = gathered <= gather_limit and mesh.shape["local"] == 2 and rest[0].shape[1] == mesh.shape["node"]
        body = gather_shards if fits else shards
        return jax.shard_map(body, mesh=mesh, in_specs=in_specs, out_specs=out_specs, check_vma=False)(d_out, *rest)

    return run
```
